256 devices in a mesh: cp: 32 (over z, x), dp: 8 (over y, core).
Axes of the slice: x: 4, y: 4, z: 8, core: 2. Of those that a mesh axis runs over, the one named last changes fastest.
Arguments:
- llm_grads: bfloat16 [8, 1536, 8192], P('dp', 'cp'), may hold values from -6 to 6
- llm_owner: int32 [8, 1536], P('dp', 'cp'), may hold values from 0 to 1535, as said below
- image_ids: int32 [8, 1536], P('dp'), may hold values from 0 to 63, never falling along the last dimension, each value on 1 to 48 neighbouring positions
- stream: bfloat16 [8, 6144, 1280], P('dp', 'cp'), may hold values from -6 to 6
- ln_gain: float32 [1280], replicated, may hold values from 0.1 to 1.9
- pre_act: bfloat16 [8, 1536, 2560], P(None, 'cp', 'dp'), may hold values from -6 to 6
- w_in: bfloat16 [5120, 2560], P(None, 'dp'), may hold values from -0.078125 to 0.078125
- w_out: bfloat16 [2560, 8192], P('dp'), may hold values from -0.125 to 0.125
- qkv: bfloat16 [8, 6144, 3840], P('dp', 'cp'), may hold values from -5 to 5
- w_proj: bfloat16 [1280, 1280], P('cp'), may hold values from -0.15625 to 0.15625
Outputs:
- d_stream: bfloat16 [8, 6144, 1280], P('dp', 'cp')
- d_qkv: bfloat16 [8, 6144, 3840], P('dp', 'cp')
- d_proj: float32 [1280, 1280], P('cp')
- d_gain: float32 [1280], replicated
The draws below stay inside these ranges and needn't reach their ends.
Inputs may be any that keep to these rules, and one draw needn't show every extreme that they name: Each row of llm_owner is a permutation of the 1536 merged tokens. The rows of one index of cp (aligned blocks of 48) send either exactly 3 or no rows to each block of 48 merged tokens.
All inputs are finite; a program needn't handle non-finite values.
Results may differ from the reference program's by a relative error of at most 0.033.
Values may be sent and summed in bfloat16 or wider, within the bound.
No kernel may reach another device: no remote copies, remote signals or barrier semaphores. Data moves between devices by JAX's collectives and lax.ppermute only.
A program may use at most 128 MiB of HBM per device.

```python
import math
import jax
import jax.numpy as jnp
import numpy as np
from jax import lax

D_VIT = 1280
HEADS = 16
HEAD_DIM = 80
D_LLM = 8192
HID_WIN = 2560
M_DEV = 48
MERGE_IN = 5120
P_DEV = 192
BATCHES = 8
NM = 1536
NP = 6144
CAP = 3
N_CP = 32
N_DP = 8


def draw_llm_owner(key, part):
    key = jax.random.fold_in(key, 11)
    shards = NM // M_DEV
    groups = M_DEV // CAP

    def one_batch(batch_key):
        offsets = jax.random.permutation(jax.random.fold_in(batch_key, 1), shards)[:groups]
        orders = jax.vmap(lambda shard: jax.random.permutation(jax.random.fold_in(batch_key, 1000 + shard), M_DEV))(jnp.arange(shards))
        senders = jnp.arange(shards)[:, None, None]
        group_ids = jnp.arange(groups)[None, :, None]
        within = jnp.arange(CAP)[None, None, :]
        source = (senders - offsets[None, :, None]) % shards
        tokens_sent = source * M_DEV + orders[source, group_ids * CAP + within]
        flat_owner = tokens_sent.reshape(shards, M_DEV)
        mixing = jax.vmap(lambda shard: jax.random.permutation(jax.random.fold_in(batch_key, 5000 + shard), M_DEV))(jnp.arange(shards))
        return jnp.take_along_axis(flat_owner, mixing, axis=1).reshape(-1)
    owners = jax.vmap(lambda batch: one_batch(jax.random.fold_in(key, batch)))(jnp.arange(BATCHES))
    return owners.astype(jnp.int32)


def draw_qkv(key, part):
    key = jax.random.fold_in(key, 23)
    shape = (BATCHES, NP, 3 * D_VIT)
    values_drawn = jnp.clip(jax.random.normal(key, shape, jnp.float32), -4.0, 4.0)
    return values_drawn.astype(jnp.bfloat16)


def block_levels(rng, extent, pieces, low, high):
    def one(dim, parts):
        draws = jax.random.uniform(jax.random.fold_in(jax.random.fold_in(rng, 6), dim), (parts,), jnp.float32, low / len(pieces), high / len(pieces))
        return jnp.repeat(jnp.exp(draws), extent[dim] // parts).reshape((-1,) + (1,) * (len(extent) - dim - 1))

    level = one(*pieces[0])
    for cut in pieces[1:]:
        level = level * one(*cut)
    return level


def length_profile(number_of, total, limit, skew):
    portions = [(1 << 20) // math.isqrt(grade ** skew) + 1 for grade in range(2, number_of + 1)]
    rest, holding = total - limit - (number_of - 1), [1] * (number_of - 1)
    while rest > 0:
        movable = [i for i in range(number_of - 1) if holding[i] < limit]
        pool, budget = sum([portions[i] for i in movable]), rest
        for i in movable:
            more = min(limit - holding[i], max(1, budget * portions[i] // pool), rest)
            holding[i] = holding[i] + more
            rest = rest - more
    return np.array([limit] + holding)


def ragged_sizes(own_key, count, total, most, lean):
    if count == 2:
        one = jax.random.randint(own_key, (), max(1, total - most), min(most, total - 1) + 1)
        return jnp.stack([one, total - one])
    sizes = jnp.asarray(length_profile(count, total, most, lean), jnp.int32)
    couples = (count - 1) // 2
    giver, receiver = sizes[1:1 + 2 * couples:2], sizes[2:2 + 2 * couples:2]
    room = jnp.minimum(giver - 1, most - receiver)
    shifted = jax.random.randint(jax.random.fold_in(own_key, 1), (couples,), 0, 1 << 20) % (room + 1)
    sizes = sizes.at[1:1 + 2 * couples:2].set(giver - shifted).at[2:2 + 2 * couples:2].set(receiver + shifted)
    return sizes[jax.random.permutation(jax.random.fold_in(own_key, 2), count)]


def centred(stream_key, shape, deviation, bound, pieces=(), kind=jnp.bfloat16):
    entries = jax.random.normal(stream_key, shape, jnp.float32) * deviation
    if len(pieces) > 0:
        entries = block_levels(stream_key, shape, pieces, -0.22, 0.18) * entries
    return jnp.clip(entries, min=-bound, max=bound).astype(kind)


def setup_inputs(seed: int = 0) -> dict:
    arg_keys = jax.random.split(jax.random.key(seed), 11)
    return {
        "llm_grads": centred(arg_keys[0], (BATCHES, NM, D_LLM), 1.0, 6.0, ((0, 8), (1, 32))),
        "llm_owner": draw_llm_owner(jax.random.fold_in(arg_keys[10], 71), 0),
        "image_ids": jax.vmap(lambda own: jnp.searchsorted(jnp.cumsum(ragged_sizes(own, 2 * NM // M_DEV, NM, M_DEV, 2)), jnp.arange(NM), side="right"))(jax.random.split(arg_keys[2], BATCHES)).reshape((BATCHES, NM)).astype(jnp.int32),
        "stream": centred(arg_keys[3], (BATCHES, NP, D_VIT), 1.0, 6.0, ((0, 8), (1, 32))),
        "ln_gain": jnp.clip(1.0 + 0.18 * jax.random.normal(arg_keys[4], (D_VIT,), jnp.float32), 0.1, 1.9),
        "pre_act": centred(arg_keys[5], (BATCHES, NM, HID_WIN), 1.0, 6.0, ((1, 32), (2, 8))),
        "w_in": centred(arg_keys[6], (MERGE_IN, HID_WIN), MERGE_IN ** -0.5, 0.078125, ((1, 8),)),
        "w_out": centred(arg_keys[7], (HID_WIN, D_LLM), HID_WIN ** -0.5, 0.125, ((0, 8),)),
        "qkv": draw_qkv(jax.random.fold_in(arg_keys[10], 71), 0),
        "w_proj": centred(arg_keys[9], (D_VIT, D_VIT), D_VIT ** -0.5, 0.15625, ((0, 32),)),
    }


EPS = 1e-06

def gelu_slope(pre_value):
    normal_cdf = 0.5 * (1.0 + lax.erf(pre_value * 0.7071067811865476))
    density = jnp.exp(-0.5 * pre_value * pre_value) * 0.3989422804014327
    return normal_cdf + pre_value * density

def block_backward(queries, key_heads, value_heads, d_heads, seg_rows, seg_keys):
    single = jnp.float32
    score_scale = 1.0 / math.sqrt(queries.shape[-1])
    scores = jnp.einsum('qhe,khe->hqk', queries.astype(single), key_heads.astype(single)) * score_scale
    same_image = seg_rows[:, None] == seg_keys[None, :]
    scores = jnp.where(same_image[None], scores, -1e+30)
    row_max = lax.optimization_barrier(jnp.max(scores, axis=-1, keepdims=True))
    weights = jnp.exp(scores - row_max)
    probs = weights / lax.optimization_barrier(jnp.sum(weights, axis=-1, keepdims=True))
    probs_low = lax.optimization_barrier(probs.astype(jnp.bfloat16))
    attention = jnp.einsum('hqk,khe->qhe', probs_low.astype(single), value_heads.astype(single))
    attention = lax.optimization_barrier(attention.astype(jnp.bfloat16))
    d_probs = jnp.einsum('qhe,khe->hqk', d_heads.astype(single), value_heads.astype(single))
    row_delta = jnp.einsum('qhe,qhe->hq', d_heads.astype(single), attention.astype(single))
    d_scores = probs * (d_probs - row_delta[:, :, None]) * score_scale
    d_scores = lax.optimization_barrier(d_scores.astype(jnp.bfloat16))
    d_query = jnp.einsum('hqk,khe->qhe', d_scores.astype(single), key_heads.astype(single))
    d_keys = jnp.einsum('hqk,qhe->khe', d_scores.astype(single), queries.astype(single))
    d_values = jnp.einsum('hqk,qhe->khe', probs_low.astype(single), d_heads.astype(single))
    return (attention, d_query, d_keys, d_values)

def reference(llm_grads, llm_owner, image_ids, stream, ln_gain, pre_act, w_in, w_out, qkv, w_proj):
    single = jnp.float32
    batches = llm_grads.shape[0]
    width_llm = llm_grads.shape[2]
    patches = stream.shape[1]
    width = stream.shape[2]
    hidden = w_out.shape[0]
    group_width = hidden // N_DP

    def place_rows(grad_rows, owner_ids):
        return jnp.zeros_like(grad_rows).at[owner_ids].set(grad_rows)
    routed = jax.vmap(place_rows)(llm_grads, llm_owner)
    d_hidden = jnp.dot(routed.reshape(-1, width_llm), w_out.T, preferred_element_type=single)
    d_pre = d_hidden * gelu_slope(pre_act.reshape(-1, hidden).astype(single))
    d_pre = lax.optimization_barrier(d_pre.astype(jnp.bfloat16))
    d_norm = jnp.zeros((d_pre.shape[0], w_in.shape[0]), single)
    for group in range(N_DP):
        low = group * group_width
        partial_sum = jnp.dot(d_pre[:, low:low + group_width], w_in[:, low:low + group_width].T, preferred_element_type=single)
        partial_sum = lax.optimization_barrier(partial_sum.astype(jnp.bfloat16))
        d_norm = d_norm + partial_sum.astype(single)
    d_norm = d_norm.reshape(batches, patches, width)
    stream_wide = stream.astype(single)
    inverse = lax.rsqrt(lax.optimization_barrier(jnp.mean(stream_wide * stream_wide, axis=-1, keepdims=True)) + EPS)
    normed = stream_wide * inverse
    d_gain = lax.optimization_barrier(jnp.sum(d_norm * normed, axis=(0, 1)))
    d_normed = d_norm * ln_gain
    d_stream = inverse * (d_normed - normed * lax.optimization_barrier(jnp.mean(d_normed * normed, axis=-1, keepdims=True)))
    d_stream = lax.optimization_barrier(d_stream.astype(jnp.bfloat16))
    d_out = jnp.dot(d_stream.reshape(-1, width), w_proj.T, preferred_element_type=single)
    d_out = lax.optimization_barrier(d_out.astype(jnp.bfloat16)).reshape(batches, patches, width)
    segments = jnp.repeat(image_ids, 4, axis=1).astype(jnp.int32)

    def one_batch(inputs):
        batch_qkv, segment, batch_dout = inputs
        queries = batch_qkv[:, :width].reshape(patches, HEADS, HEAD_DIM)
        key_heads = batch_qkv[:, width:2 * width].reshape(patches, HEADS, HEAD_DIM)
        value_heads = batch_qkv[:, 2 * width:].reshape(patches, HEADS, HEAD_DIM)
        d_heads = batch_dout.reshape(patches, HEADS, HEAD_DIM)
        zero_rim = jnp.zeros((P_DEV, HEADS, HEAD_DIM), jnp.bfloat16)
        keys_pad = jnp.concatenate([zero_rim, key_heads, zero_rim], axis=0)
        values_pad = jnp.concatenate([zero_rim, value_heads, zero_rim], axis=0)
        seg_rim = jnp.full((P_DEV,), -1, jnp.int32)
        seg_pad = jnp.concatenate([seg_rim, segment, seg_rim], axis=0)
        empty = jnp.zeros((patches + 2 * P_DEV, HEADS, HEAD_DIM), jnp.float32)

        def step(carry, block_id):
            key_total, value_total = carry
            offset = (block_id * P_DEV).astype(jnp.int32)
            q_block = lax.dynamic_slice_in_dim(queries, offset, P_DEV, 0)
            dout_block = lax.dynamic_slice_in_dim(d_heads, offset, P_DEV, 0)
            seg_block = lax.dynamic_slice_in_dim(segment, offset, P_DEV, 0)
            key_window = lax.dynamic_slice_in_dim(keys_pad, offset, 3 * P_DEV, 0)
            value_window = lax.dynamic_slice_in_dim(values_pad, offset, 3 * P_DEV, 0)
            seg_window = lax.dynamic_slice_in_dim(seg_pad, offset, 3 * P_DEV, 0)
            attention, d_query, d_keys, d_values = block_backward(q_block, key_window, value_window, dout_block, seg_block, seg_window)
            key_total = lax.dynamic_update_slice_in_dim(key_total, lax.dynamic_slice_in_dim(key_total, offset, 3 * P_DEV, 0) + d_keys, offset, 0)
            value_total = lax.dynamic_update_slice_in_dim(value_total, lax.dynamic_slice_in_dim(value_total, offset, 3 * P_DEV, 0) + d_values, offset, 0)
            return ((key_total, value_total), (attention, d_query))
        (key_total, value_total), (attention, d_query) = lax.scan(step, (empty, empty), jnp.arange(N_CP, dtype=jnp.int32))
        d_keys = key_total[P_DEV:P_DEV + patches].reshape(patches, width)
        d_values = value_total[P_DEV:P_DEV + patches].reshape(patches, width)
        packed = jnp.concatenate([d_query.reshape(patches, width), d_keys, d_values], axis=1)
        return (attention.reshape(patches, width), packed.astype(jnp.bfloat16))
    attention_all, d_qkv = lax.map(one_batch, (qkv, segments, d_out))
    attention_blocks = attention_all.reshape(-1, P_DEV, width)
    stream_blocks = d_stream.reshape(-1, P_DEV, width)

    def add_block(total, pair):
        attention_block, stream_block = pair
        partial_sum = jnp.dot(attention_block.T, stream_block, preferred_element_type=single)
        partial_sum = lax.optimization_barrier(partial_sum.astype(jnp.bfloat16))
        return (total + partial_sum.astype(single), None)
    d_proj, _ = lax.scan(add_block, jnp.zeros((width, width), single), (attention_blocks, stream_blocks))
    return (d_stream, d_qkv, d_proj, d_gain)
```

```python
import math

import jax
import jax.numpy as jnp
from jax import lax
from jax.sharding import PartitionSpec as P

HEADS = 16
HEAD_DIM = 80


EPS = 1e-06


def extended(block, sides, width):
    for axis, dim in sides:
        count = lax.axis_size(axis)
        forward = [(i, i + 1) for i in range(count - 1)]
        backward = [(target, source) for source, target in forward]
        low = lax.ppermute(
            lax.slice_in_dim(block, block.shape[dim] - width, None, axis=dim), axis, forward
        )
        high = lax.ppermute(lax.slice_in_dim(block, 0, width, axis=dim), axis, backward)
        block = jnp.concatenate([low, block, high], axis=dim)
    return block


def from_behind(block, axis, distance):
    devices = range(lax.axis_size(axis))
    route = [(i - distance, i) for i in devices if i - distance in devices]
    return lax.ppermute(block, axis, route)


def gelu_slope(pre_value):
    normal_cdf = 0.5 * (1.0 + lax.erf(pre_value * 0.7071067811865476))
    density = jnp.exp(-0.5 * pre_value * pre_value) * 0.3989422804014327
    return normal_cdf + pre_value * density


def block_backward(queries, key_heads, value_heads, d_heads, seg_rows, seg_keys):
    single = jnp.float32
    narrow = jnp.bfloat16
    score_scale = 1.0 / math.sqrt(queries.shape[-1])
    scores = (
        jnp.einsum("qhe,khe->hqk", queries, key_heads, preferred_element_type=single) * score_scale
    )
    same_image = seg_rows[:, None] == seg_keys[None, :]
    scores = jnp.where(same_image[None], scores, -1e30)
    row_max = jnp.max(scores, axis=-1, keepdims=True)
    weights = jnp.exp(scores - row_max)
    probs = weights / jnp.sum(weights, axis=-1, keepdims=True)
    probs_low = probs.astype(narrow)
    attention = jnp.einsum(
        "hqk,khe->qhe", probs_low, value_heads, preferred_element_type=single
    ).astype(narrow)
    d_probs = jnp.einsum("qhe,khe->hqk", d_heads, value_heads, preferred_element_type=single)
    row_delta = jnp.einsum("qhe,qhe->hq", d_heads, attention, preferred_element_type=single)
    d_scores = (probs * (d_probs - row_delta[:, :, None]) * score_scale).astype(narrow)
    d_query = jnp.einsum("hqk,khe->qhe", d_scores, key_heads, preferred_element_type=single)
    d_keys = jnp.einsum("hqk,qhe->khe", d_scores, queries, preferred_element_type=single)
    d_values = jnp.einsum("hqk,qhe->khe", probs_low, d_heads, preferred_element_type=single)
    return (attention, d_query, d_keys, d_values)


def local(llm_grads, llm_owner, image_ids, stream, ln_gain, pre_act, w_in, w_out, qkv, w_proj):
    single = jnp.float32
    narrow = jnp.bfloat16
    shards = lax.axis_size("cp")
    batches = lax.axis_size("dp")
    device_index = lax.axis_index("cp")
    row_count = llm_grads.shape[1]
    patches = stream.shape[1]
    width = stream.shape[2]
    hidden = w_out.shape[0]
    slot_count = 2 * row_count // shards
    rows = batches * row_count
    packed_width = -(-(hidden + 1) // 128) * 128
    owners = lax.all_gather(llm_owner[0], "dp", axis=0)
    gathered = lax.all_gather(llm_grads[0], "dp", axis=0, tiled=True)
    full_proj = lax.all_gather(w_proj, "cp", axis=0, tiled=True)
    target = owners // row_count
    place = (owners % row_count).reshape(rows, 1)
    same_target = target[:, :, None] == target[:, None, :]
    before = jnp.arange(row_count)[None, :] < jnp.arange(row_count)[:, None]
    rank = jnp.sum((same_target & before[None]).astype(jnp.int32), axis=2)
    batch_of = jnp.arange(batches, dtype=jnp.int32)[:, None]
    slot = ((target * batches + batch_of) * slot_count + rank).reshape(1, rows)
    slots = shards * batches * slot_count
    pick = (jnp.arange(slots, dtype=jnp.int32)[:, None] == slot).astype(narrow)
    d_rows = jnp.dot(gathered, w_out.T, preferred_element_type=single).astype(narrow)
    tags = jnp.where(
        jnp.arange(packed_width - hidden)[None, :] == 0, place + 1, 0
    ).astype(narrow)
    outgoing = jnp.dot(
        pick, jnp.concatenate([d_rows, tags], axis=1), preferred_element_type=single
    ).astype(narrow)
    arrived = lax.all_to_all(
        outgoing.reshape(shards, batches * slot_count, packed_width),
        "cp",
        split_axis=0,
        concat_axis=0,
        tiled=True,
    ).reshape(slots, packed_width)
    tag_row = arrived[:, hidden].astype(jnp.int32).reshape(1, slots)
    slot_batch = (jnp.arange(slots, dtype=jnp.int32) // slot_count % batches)[None, :]
    home = jnp.where(tag_row > 0, slot_batch * row_count + tag_row - 1, -1)
    settle = (jnp.arange(rows, dtype=jnp.int32)[:, None] == home).astype(narrow)
    d_hidden = jnp.dot(settle, arrived, preferred_element_type=single)[:, :hidden].reshape(
        batches, row_count, hidden
    )
    saved_pre = pre_act.astype(single)
    d_pre = (d_hidden * gelu_slope(saved_pre)).astype(narrow)
    partials = jnp.einsum("bmh,ih->bmi", d_pre, w_in, preferred_element_type=single)
    d_norm = (
        lax.psum_scatter(partials.astype(jnp.bfloat16), "dp", scatter_dimension=0, tiled=True)
        .astype(jnp.float32)
        .reshape(patches, width)
    )
    stream_wide = stream[0].astype(single)
    inverse = lax.rsqrt(jnp.mean(stream_wide * stream_wide, axis=-1, keepdims=True) + EPS)
    normed = stream_wide * inverse
    gain_part = jnp.sum(d_norm * normed, axis=0)
    d_normed = d_norm * ln_gain
    d_stream = (
        inverse * (d_normed - normed * jnp.mean(d_normed * normed, axis=-1, keepdims=True))
    ).astype(narrow)
    d_out = jnp.einsum(
        "pj,ij->pi",
        d_stream,
        full_proj,
        preferred_element_type=single,
    ).astype(narrow)
    queries = qkv[0, :, :width].reshape(patches, HEADS, HEAD_DIM)
    key_values = extended(qkv[0, :, width:], (("cp", 0),), patches)
    key_heads = key_values[:, :width].reshape(3 * patches, HEADS, HEAD_DIM)
    value_heads = key_values[:, width:].reshape(3 * patches, HEADS, HEAD_DIM)
    segment = jnp.repeat(image_ids[0], 4)
    seg_rim = jnp.full((patches,), -1, jnp.int32)
    seg_pad = jnp.concatenate([seg_rim, segment, seg_rim], axis=0)
    seg_keys = lax.dynamic_slice_in_dim(seg_pad, device_index * patches, 3 * patches, 0)
    seg_rows = lax.dynamic_slice_in_dim(segment, device_index * patches, patches, 0)
    attention, d_query, d_keys, d_values = block_backward(
        queries, key_heads, value_heads, d_out.reshape(patches, HEADS, HEAD_DIM), seg_rows, seg_keys
    )
    d_pairs = jnp.concatenate(
        [d_keys.reshape(3 * patches, width), d_values.reshape(3 * patches, width)], axis=1
    )
    from_prev = from_behind(d_pairs[2 * patches :].astype(jnp.bfloat16), "cp", 1).astype(
        jnp.float32
    )
    from_next = from_behind(d_pairs[:patches].astype(jnp.bfloat16), "cp", -1).astype(jnp.float32)
    own_part = d_pairs[patches : 2 * patches] + from_prev + from_next
    d_qkv = jnp.concatenate([d_query.reshape(patches, width), own_part], axis=1).astype(narrow)
    share = width // shards
    part = share // batches
    features = attention.reshape(patches, shards, batches, part)
    features = features.transpose(0, 2, 1, 3).reshape(patches, width)
    d_proj_part = jnp.einsum("pi,pj->ij", features, d_stream, preferred_element_type=single)
    over_batches = lax.psum_scatter(
        d_proj_part.astype(narrow), "dp", scatter_dimension=0, tiled=True
    )
    own_rows = lax.psum_scatter(
        over_batches.reshape(shards, part, width), "cp", scatter_dimension=0, tiled=True
    )
    d_proj = lax.all_gather(own_rows[0], "dp", axis=0, tiled=True).astype(single)
    d_gain = lax.psum(gain_part, ("cp", "dp"))
    return (d_stream[None], d_qkv[None], d_proj, d_gain)


def solution(mesh):
    in_specs = (
        P("dp", "cp", None),
        P("dp", "cp"),
        P("dp", None),
        P("dp", "cp", None),
        P(),
        P(None, "cp", "dp"),
        P(None, "dp"),
        P("dp", None),
        P("dp", "cp", None),
        P("cp", None),
    )
    out_specs = (P("dp", "cp", None), P("dp", "cp", None), P("cp", None), P())
    return jax.shard_map(local, mesh=mesh, in_specs=in_specs, out_specs=out_specs, check_vma=False)
```

```python
import math

import jax
import jax.numpy as jnp
from jax import lax
from jax.sharding import PartitionSpec as P

HEADS = 16
HEAD_DIM = 80


EPS = 1e-06


def extended(block, sides, width):
    for axis, dim in sides:
        count = lax.axis_size(axis)
        forward = [(i, i + 1) for i in range(count - 1)]
        backward = [(target, source) for source, target in forward]
        low = lax.ppermute(
            lax.slice_in_dim(block, block.shape[dim] - width, None, axis=dim), axis, forward
        )
        high = lax.ppermute(lax.slice_in_dim(block, 0, width, axis=dim), axis, backward)
        block = jnp.concatenate([low, block, high], axis=dim)
    return block


def from_behind(block, axis, distance):
    devices = range(lax.axis_size(axis))
    route = [(i - distance, i) for i in devices if i - distance in devices]
    return lax.ppermute(block, axis, route)


def gelu_slope(pre_value):
    normal_cdf = 0.5 * (1.0 + lax.erf(pre_value * 0.7071067811865476))
    density = jnp.exp(-0.5 * pre_value * pre_value) * 0.3989422804014327
    return normal_cdf + pre_value * density


def in_parts(vector):
    parts = []
    for _ in range(3):
        part = lax.reduce_precision(vector, 8, 7)
        parts.append(part.astype(jnp.bfloat16))
        vector = vector - part
    return jnp.stack(parts)


def block_forward(queries, key_heads, value_heads, seg_rows, seg_keys):
    single = jnp.float32
    narrow = jnp.bfloat16
    score_scale = 1.0 / math.sqrt(queries.shape[-1])
    scores = (
        jnp.einsum("qhe,khe->hqk", queries, key_heads, preferred_element_type=single) * score_scale
    )
    same_image = seg_rows[:, None] == seg_keys[None, :]
    scores = jnp.where(same_image[None], scores, -1e30)
    row_max = jnp.max(scores, axis=-1, keepdims=True)
    weights = jnp.exp(scores - row_max)
    probs = weights / jnp.sum(weights, axis=-1, keepdims=True)
    probs_low = probs.astype(narrow)
    attention = jnp.einsum(
        "hqk,khe->qhe", probs_low, value_heads, preferred_element_type=single
    ).astype(narrow)
    return (probs, probs_low, attention)


def block_backward(queries, key_heads, value_heads, d_heads, probs, probs_low, attention):
    single = jnp.float32
    narrow = jnp.bfloat16
    score_scale = 1.0 / math.sqrt(queries.shape[-1])
    d_probs = jnp.einsum("qhe,khe->hqk", d_heads, value_heads, preferred_element_type=single)
    row_delta = jnp.einsum("qhe,qhe->hq", d_heads, attention, preferred_element_type=single)
    d_scores = (probs * (d_probs - row_delta[:, :, None]) * score_scale).astype(narrow)
    d_query = jnp.einsum("hqk,khe->qhe", d_scores, key_heads, preferred_element_type=single)
    d_keys = jnp.einsum("hqk,qhe->khe", d_scores, queries, preferred_element_type=single)
    d_values = jnp.einsum("hqk,qhe->khe", probs_low, d_heads, preferred_element_type=single)
    return (d_query, d_keys, d_values)


def local(llm_grads, llm_owner, image_ids, stream, ln_gain, pre_act, w_in, w_out, qkv, w_proj):
    single = jnp.float32
    narrow = jnp.bfloat16
    shards = lax.axis_size("cp")
    batches = lax.axis_size("dp")
    device_index = lax.axis_index("cp")
    row_count = llm_grads.shape[1]
    patches = stream.shape[1]
    width = stream.shape[2]
    hidden = w_out.shape[0]
    slot_count = 2 * row_count // shards
    rows = batches * row_count
    packed_width = -(-(hidden + 1) // 128) * 128
    owners = lax.all_gather(llm_owner[0], "dp", axis=0)
    gathered = lax.all_gather(llm_grads[0], "dp", axis=0, tiled=True)
    share = w_proj.shape[0]
    part = share // batches
    own_proj = lax.dynamic_slice_in_dim(w_proj, lax.axis_index("dp") * part, part, 0)
    proj_parts = lax.all_to_all(
        jnp.broadcast_to(own_proj[None], (shards, part, width)),
        "cp",
        split_axis=0,
        concat_axis=0,
        tiled=True,
    ).reshape(shards * part, width)
    queries = qkv[0, :, :width].reshape(patches, HEADS, HEAD_DIM)
    key_values = extended(qkv[0, :, width:], (("cp", 0),), patches)
    gathered, key_values, proj_parts = lax.optimization_barrier(
        (gathered, key_values, proj_parts)
    )
    full_proj = lax.all_gather(proj_parts, "dp", axis=0, tiled=True)
    full_proj = full_proj.reshape(batches, shards, part, width)
    full_proj = full_proj.transpose(1, 0, 2, 3).reshape(width, width)
    target = owners // row_count
    place = (owners % row_count).reshape(rows, 1)
    same_target = target[:, :, None] == target[:, None, :]
    before = jnp.arange(row_count)[None, :] < jnp.arange(row_count)[:, None]
    rank = jnp.sum((same_target & before[None]).astype(jnp.int32), axis=2)
    batch_of = jnp.arange(batches, dtype=jnp.int32)[:, None]
    slot = ((target * batches + batch_of) * slot_count + rank).reshape(1, rows)
    slots = shards * batches * slot_count
    pick = (jnp.arange(slots, dtype=jnp.int32)[:, None] == slot).astype(narrow)
    d_rows = jnp.dot(gathered, w_out.T, preferred_element_type=single).astype(narrow)
    tags = jnp.where(
        jnp.arange(packed_width - hidden)[None, :] == 0, place + 1, 0
    ).astype(narrow)
    outgoing = jnp.dot(
        pick, jnp.concatenate([d_rows, tags], axis=1), preferred_element_type=single
    ).astype(narrow)
    arrived = lax.all_to_all(
        outgoing.reshape(shards, batches * slot_count, packed_width),
        "cp",
        split_axis=0,
        concat_axis=0,
        tiled=True,
    ).reshape(slots, packed_width)
    arrived, full_proj = lax.optimization_barrier((arrived, full_proj))
    tag_row = arrived[:, hidden].astype(jnp.int32).reshape(1, slots)
    slot_batch = (jnp.arange(slots, dtype=jnp.int32) // slot_count % batches)[None, :]
    home = jnp.where(tag_row > 0, slot_batch * row_count + tag_row - 1, -1)
    settle = (jnp.arange(rows, dtype=jnp.int32)[:, None] == home).astype(narrow)
    d_hidden = jnp.dot(settle, arrived, preferred_element_type=single)[:, :hidden].reshape(
        batches, row_count, hidden
    )
    saved_pre = pre_act.astype(single)
    d_pre = (d_hidden * gelu_slope(saved_pre)).astype(narrow)
    partials = jnp.einsum("bmh,ih->bmi", d_pre, w_in, preferred_element_type=single)
    d_norm = lax.psum_scatter(partials.astype(narrow), "dp", scatter_dimension=0, tiled=True)
    key_heads = key_values[:, :width].reshape(3 * patches, HEADS, HEAD_DIM)
    value_heads = key_values[:, width:].reshape(3 * patches, HEADS, HEAD_DIM)
    segment = jnp.repeat(image_ids[0], 4)
    seg_rim = jnp.full((patches,), -1, jnp.int32)
    seg_pad = jnp.concatenate([seg_rim, segment, seg_rim], axis=0)
    seg_keys = lax.dynamic_slice_in_dim(seg_pad, device_index * patches, 3 * patches, 0)
    seg_rows = lax.dynamic_slice_in_dim(segment, device_index * patches, patches, 0)
    probs, probs_low, attention = block_forward(
        queries, key_heads, value_heads, seg_rows, seg_keys
    )
    features = attention.reshape(patches, shards, batches, part)
    features = features.transpose(0, 2, 1, 3).reshape(patches, width)
    stream_wide = stream[0].astype(single)
    inverse = lax.rsqrt(jnp.mean(stream_wide * stream_wide, axis=-1, keepdims=True) + EPS)
    normed = stream_wide * inverse
    d_norm, features = lax.optimization_barrier((d_norm, features))
    d_norm = d_norm.astype(single).reshape(patches, width)
    gain_part = jnp.sum(d_norm * normed, axis=0)
    d_normed = d_norm * ln_gain
    d_stream = (
        inverse * (d_normed - normed * jnp.mean(d_normed * normed, axis=-1, keepdims=True))
    ).astype(narrow)
    d_proj_part = jnp.einsum(
        "pi,pj->ij", features, d_stream, preferred_element_type=single
    ).astype(narrow)
    d_proj_part, d_stream = lax.optimization_barrier((d_proj_part, d_stream))
    over_batches = lax.psum_scatter(d_proj_part, "dp", scatter_dimension=0, tiled=True)
    d_out = jnp.einsum(
        "pj,ij->pi", d_stream, full_proj, preferred_element_type=single
    ).astype(narrow)
    d_query, d_keys, d_values = block_backward(
        queries,
        key_heads,
        value_heads,
        d_out.reshape(patches, HEADS, HEAD_DIM),
        probs,
        probs_low,
        attention,
    )
    d_pairs = jnp.concatenate(
        [d_keys.reshape(3 * patches, width), d_values.reshape(3 * patches, width)], axis=1
    )
    from_prev = from_behind(d_pairs[2 * patches :].astype(jnp.bfloat16), "cp", 1).astype(
        jnp.float32
    )
    from_next = from_behind(d_pairs[:patches].astype(jnp.bfloat16), "cp", -1).astype(jnp.float32)
    own_part = d_pairs[patches : 2 * patches] + from_prev + from_next
    d_qkv = jnp.concatenate([d_query.reshape(patches, width), own_part], axis=1).astype(narrow)
    spread = jnp.concatenate(
        [
            over_batches.reshape(shards, part, width),
            jnp.broadcast_to(in_parts(gain_part)[None], (shards, 3, width)),
        ],
        axis=1,
    )
    per_shard = lax.all_to_all(spread, "cp", split_axis=0, concat_axis=0, tiled=True)
    totals = jnp.sum(per_shard.astype(single), axis=0)
    own_rows = jnp.concatenate(
        [totals[:part].astype(narrow), in_parts(jnp.sum(totals[part:], axis=0))], axis=0
    )
    whole = lax.all_gather(own_rows, "dp", axis=0).astype(single)
    d_proj = whole[:, :part].reshape(share, width)
    d_gain = jnp.sum(whole[:, part:], axis=(0, 1))
    return (d_stream[None], d_qkv[None], d_proj, d_gain)


def solution(mesh):
    in_specs = (
        P("dp", "cp", None),
        P("dp", "cp"),
        P("dp", None),
        P("dp", "cp", None),
        P(),
        P(None, "cp", "dp"),
        P(None, "dp"),
        P("dp", None),
        P("dp", "cp", None),
        P("cp", None),
    )
    out_specs = (P("dp", "cp", None), P("dp", "cp", None), P("cp", None), P())
    return jax.shard_map(local, mesh=mesh, in_specs=in_specs, out_specs=out_specs, check_vma=False)
```

```python
import math

import jax
import jax.numpy as jnp
from jax import lax
from jax.experimental import pallas as pl
from jax.experimental.pallas import tpu as pltpu
from jax.sharding import PartitionSpec as P

HEADS = 16
HEAD_DIM = 80


EPS = 1e-06


def from_behind(block, axis, distance):
    devices = range(lax.axis_size(axis))
    route = [(i - distance, i) for i in devices if i - distance in devices]
    return lax.ppermute(block, axis, route)


def by_core(block, dim, own):
    core = lax.axis_index("dp") % 2
    return lax.dynamic_index_in_dim(block, core if own else 1 - core, dim, keepdims=False)


def added_on_chip(partial_of):
    count = lax.axis_size("dp")
    swap = [(i, i ^ 1) for i in range(count)]
    received = lax.ppermute(partial_of(False).astype(jnp.bfloat16), "dp", swap)
    return (partial_of(True) + received.astype(jnp.float32)).astype(jnp.bfloat16)


def scattered_over_y(pair):
    count = lax.axis_size("dp")
    groups = [list(range(core, count, 2)) for core in range(2)]
    return lax.psum_scatter(
        pair, "dp", scatter_dimension=0, axis_index_groups=groups, tiled=True
    )


def gelu_slope(pre_value):
    normal_cdf = 0.5 * (1.0 + lax.erf(pre_value * 0.7071067811865476))
    density = jnp.exp(-0.5 * pre_value * pre_value) * 0.3989422804014327
    return normal_cdf + pre_value * density


def in_parts(vector):
    parts = []
    for _ in range(3):
        part = lax.reduce_precision(vector, 8, 7)
        parts.append(part.astype(jnp.bfloat16))
        vector = vector - part
    return jnp.stack(parts)


GROUP = 8
CONTRACT_LAST = (((1,), (1,)), ((), ()))
CONTRACT_FIRST = (((0,), (0,)), ((), ()))
CONTRACT_INNER = (((1,), (0,)), ((), ()))


def mxu(a, b, dims):
    return lax.dot_general(a, b, dims, preferred_element_type=jnp.float32)


def head_columns(ref, head):
    return ref[..., head * HEAD_DIM : (head + 1) * HEAD_DIM]


def window(low_ref, own_ref, high_ref, head):
    parts = [head_columns(low_ref, head), head_columns(own_ref, head)[0]]
    return jnp.concatenate(parts + [head_columns(high_ref, head)], axis=0)


def forward_kernel(q_ref, k_ref, v_ref, kl_ref, vl_ref, kh_ref, vh_ref, rows_ref, keys_ref,
                   att_ref, lse_ref):
    scale = 1.0 / math.sqrt(HEAD_DIM)
    mask = rows_ref[...] == keys_ref[...]
    outs = []
    stats = []
    for head in range(GROUP):
        queries = head_columns(q_ref, head)[0]
        key_heads = window(kl_ref, k_ref, kh_ref, head)
        value_heads = window(vl_ref, v_ref, vh_ref, head)
        scores = jnp.where(mask, mxu(queries, key_heads, CONTRACT_LAST) * scale, -1e30)
        row_max = jnp.max(scores, axis=-1, keepdims=True)
        weights = jnp.exp(scores - row_max)
        total = jnp.sum(weights, axis=-1, keepdims=True)
        probs_low = (weights * (1.0 / total)).astype(jnp.bfloat16)
        outs.append(mxu(probs_low, value_heads, CONTRACT_INNER).astype(jnp.bfloat16))
        stats.append(row_max + jnp.log(total))
    att_ref[...] = jnp.concatenate(outs, axis=1)
    lse_ref[0] = jnp.concatenate(stats, axis=1)


def backward_kernel(q_ref, k_ref, v_ref, kl_ref, vl_ref, kh_ref, vh_ref, rows_ref, keys_ref,
                    att_ref, lse_ref, do_ref,
                    dq_ref, low_ref, own_ref, high_ref):
    scale = 1.0 / math.sqrt(HEAD_DIM)
    narrow = jnp.bfloat16
    patches = dq_ref.shape[0]
    mask = rows_ref[...] == keys_ref[...]
    d_query = []
    d_pairs = ([], [])
    for head in range(GROUP):
        queries = head_columns(q_ref, head)[0]
        key_heads = window(kl_ref, k_ref, kh_ref, head)
        value_heads = window(vl_ref, v_ref, vh_ref, head)
        d_heads = head_columns(do_ref, head)
        scores = jnp.where(mask, mxu(queries, key_heads, CONTRACT_LAST) * scale, -1e30)
        probs = jnp.exp(scores - lse_ref[0, :, head : head + 1])
        probs_low = probs.astype(narrow)
        delta = jnp.sum(
            d_heads.astype(jnp.float32) * head_columns(att_ref, head).astype(jnp.float32),
            axis=-1,
            keepdims=True,
        )
        d_probs = mxu(d_heads, value_heads, CONTRACT_LAST)
        d_scores = (probs * ((d_probs - delta) * scale)).astype(narrow)
        d_query.append(mxu(d_scores, key_heads, CONTRACT_INNER).astype(narrow))
        d_pairs[0].append(mxu(d_scores, queries, CONTRACT_FIRST))
        d_pairs[1].append(mxu(probs_low, d_heads, CONTRACT_FIRST))
    dq_ref[...] = jnp.concatenate(d_query, axis=1)
    for i in range(2):
        total = jnp.concatenate(d_pairs[i], axis=1)
        low_ref[i] = total[:patches].astype(narrow)
        own_ref[i] = total[patches : 2 * patches]
        high_ref[i] = total[2 * patches :].astype(narrow)


def attention_calls(qkv, low, high, seg_rows, seg_keys):
    patches = qkv.shape[1]
    width = qkv.shape[2] // 3
    lanes = GROUP * HEAD_DIM
    groups = width // lanes
    own = [
        pl.BlockSpec((1, patches, lanes), lambda g, i=i: (0, 0, i * groups + g)) for i in range(3)
    ]
    halo = [
        pl.BlockSpec((patches, lanes), lambda g, i=i: (0, i * groups + g)) for i in (0, 1, 0, 1)
    ]
    ids = [
        pl.BlockSpec((patches, 1), lambda g: (0, 0)),
        pl.BlockSpec((1, 3 * patches), lambda g: (0, 0)),
    ]
    operands = (qkv, qkv, qkv, low, low, high, high, seg_rows[:, None], seg_keys[None, :])
    flat = pl.BlockSpec((patches, lanes), lambda g: (0, g))
    stat = pl.BlockSpec((1, patches, GROUP), lambda g: (g, 0, 0))
    pair = pl.BlockSpec((2, patches, lanes), lambda g: (0, 0, g))
    params = pltpu.CompilerParams(vmem_limit_bytes=48 * 1024 * 1024)
    flops = 2 * 3 * patches * patches * width
    exps = 3 * patches * patches * HEADS

    def cost(dots):
        return pl.CostEstimate(
            flops=dots * flops, bytes_accessed=12 * patches * width, transcendentals=exps
        )

    attention, stats = pl.pallas_call(
        forward_kernel,
        grid=(groups,),
        in_specs=own + halo + ids,
        out_specs=(flat, stat),
        out_shape=(
            jax.ShapeDtypeStruct((patches, width), jnp.bfloat16),
            jax.ShapeDtypeStruct((groups, patches, GROUP), jnp.float32),
        ),
        compiler_params=params,
        cost_estimate=cost(2),
        name="attention_forward",
    )(*operands)

    def backward(d_out):
        return pl.pallas_call(
            backward_kernel,
            grid=(groups,),
            in_specs=own + halo + ids + [flat, stat, flat],
            out_specs=(flat, pair, pair, pair),
            out_shape=(
                jax.ShapeDtypeStruct((patches, width), jnp.bfloat16),
                jax.ShapeDtypeStruct((2, patches, width), jnp.bfloat16),
                jax.ShapeDtypeStruct((2, patches, width), jnp.float32),
                jax.ShapeDtypeStruct((2, patches, width), jnp.bfloat16),
            ),
            compiler_params=params,
            cost_estimate=cost(5),
            name="attention_backward",
        )(*operands, attention, stats, d_out)

    return attention, backward


def local(llm_grads, llm_owner, image_ids, stream, ln_gain, pre_act, w_in, w_out, qkv, w_proj):
    single = jnp.float32
    narrow = jnp.bfloat16
    shards = lax.axis_size("cp")
    batches = lax.axis_size("dp")
    device_index = lax.axis_index("cp")
    row_count = llm_grads.shape[1]
    patches = stream.shape[1]
    width = stream.shape[2]
    hidden = w_out.shape[0]
    slot_count = 2 * row_count // shards
    rows = batches * row_count
    packed_width = -(-(hidden + 1) // 128) * 128
    owners = lax.all_gather(llm_owner[0], "dp", axis=0)
    gathered = lax.all_gather(llm_grads[0], "dp", axis=0, tiled=True)
    share = w_proj.shape[0]
    part = share // batches
    own_proj = lax.dynamic_slice_in_dim(w_proj, lax.axis_index("dp") * part, part, 0)
    own_proj, owners = lax.optimization_barrier((own_proj, owners))
    proj_parts = lax.all_to_all(
        jnp.broadcast_to(own_proj[None], (shards, part, width)),
        "cp",
        split_axis=0,
        concat_axis=0,
        tiled=True,
    ).reshape(shards * part, width)
    gathered, proj_parts = lax.optimization_barrier((gathered, proj_parts))
    full_proj = lax.all_gather(proj_parts, "dp", axis=0, tiled=True)
    low = from_behind(qkv[0, :, width:], "cp", 1)
    high = from_behind(qkv[0, :, width:], "cp", -1)
    target = owners // row_count
    place = (owners % row_count).reshape(rows, 1)
    same_target = target[:, :, None] == target[:, None, :]
    before = jnp.arange(row_count)[None, :] < jnp.arange(row_count)[:, None]
    rank = jnp.sum((same_target & before[None]).astype(jnp.int32), axis=2)
    batch_of = jnp.arange(batches, dtype=jnp.int32)[:, None]
    slot = ((target * batches + batch_of) * slot_count + rank).reshape(1, rows)
    slots = shards * batches * slot_count
    pick = (jnp.arange(slots, dtype=jnp.int32)[:, None] == slot).astype(narrow)
    d_rows = jnp.dot(gathered, w_out.T, preferred_element_type=single).astype(narrow)
    tags = jnp.where(
        jnp.arange(packed_width - hidden)[None, :] == 0, place + 1, 0
    ).astype(narrow)
    outgoing = jnp.dot(
        pick, jnp.concatenate([d_rows, tags], axis=1), preferred_element_type=single
    ).astype(narrow)
    arrived = lax.all_to_all(
        outgoing.reshape(shards, batches * slot_count, packed_width),
        "cp",
        split_axis=0,
        concat_axis=0,
        tiled=True,
    ).reshape(slots, packed_width)
    arrived, full_proj = lax.optimization_barrier((arrived, full_proj))
    tag_row = arrived[:, hidden].astype(jnp.int32).reshape(1, slots)
    slot_batch = (jnp.arange(slots, dtype=jnp.int32) // slot_count % batches)[None, :]
    home = jnp.where(tag_row > 0, slot_batch * row_count + tag_row - 1, -1)
    settle = (jnp.arange(rows, dtype=jnp.int32)[:, None] == home).astype(narrow)
    d_hidden = jnp.dot(settle, arrived, preferred_element_type=single)[:, :hidden].reshape(
        batches, row_count, hidden
    )
    saved_pre = pre_act.astype(single)
    d_pre = (d_hidden * gelu_slope(saved_pre)).astype(narrow)
    d_norm = added_on_chip(
        lambda own: (
            jnp.einsum(
                "bmh,ih->bmi",
                by_core(d_pre.reshape(batches // 2, 2, row_count, hidden), 1, own),
                w_in,
                preferred_element_type=single,
            )
        )
    )
    d_norm = scattered_over_y(d_norm)
    segment = jnp.repeat(image_ids[0], 4)
    seg_rim = jnp.full((patches,), -1, jnp.int32)
    seg_pad = jnp.concatenate([seg_rim, segment, seg_rim], axis=0)
    seg_keys = lax.dynamic_slice_in_dim(seg_pad, device_index * patches, 3 * patches, 0)
    seg_rows = lax.dynamic_slice_in_dim(segment, device_index * patches, patches, 0)
    attention, backward = attention_calls(qkv, low, high, seg_rows, seg_keys)
    features = attention.reshape(patches, shards, batches // 2, 2, part)
    features = features.transpose(0, 3, 2, 1, 4).reshape(patches, 2, width // 2)
    stream_wide = stream[0].astype(single)
    inverse = lax.rsqrt(jnp.mean(stream_wide * stream_wide, axis=-1, keepdims=True) + EPS)
    normed = stream_wide * inverse
    d_norm, features = lax.optimization_barrier((d_norm, features))
    d_norm = lax.optimization_barrier(d_norm.reshape(patches, width)).astype(single)
    gain_part = jnp.sum(d_norm * normed, axis=0)
    d_normed = d_norm * ln_gain
    d_stream = (
        inverse * (d_normed - normed * jnp.mean(d_normed * normed, axis=-1, keepdims=True))
    ).astype(narrow)
    d_stream = lax.optimization_barrier(d_stream)
    d_proj_pair = added_on_chip(
        lambda own: jnp.einsum(
            "pi,pj->ij", by_core(features, 1, own), d_stream, preferred_element_type=single
        )
    )
    d_out = jnp.einsum(
        "pj,ij->pi", d_stream, full_proj, preferred_element_type=single
    ).astype(narrow)
    row = jnp.arange(width, dtype=jnp.int32)
    natural = row // part % shards * share + row // (part * shards) * part + row % part
    order = (natural[:, None] == jnp.arange(width, dtype=jnp.int32)[None, :]).astype(narrow)
    d_out = jnp.dot(d_out, order, preferred_element_type=single).astype(narrow)
    d_proj_pair, d_out = lax.optimization_barrier((d_proj_pair, d_out))
    over_batches = scattered_over_y(d_proj_pair)
    d_query, d_low, d_own, d_high = backward(d_out)
    from_prev = from_behind(d_high, "cp", 1)
    from_next = from_behind(d_low, "cp", -1)
    spread = jnp.concatenate(
        [
            over_batches.reshape(shards, part, width),
            jnp.broadcast_to(in_parts(gain_part)[None], (shards, 3, width)),
        ],
        axis=1,
    )
    per_shard = lax.all_to_all(spread, "cp", split_axis=0, concat_axis=0, tiled=True)
    per_shard, from_prev, from_next = lax.optimization_barrier((per_shard, from_prev, from_next))
    d_pairs = (d_own + from_prev.astype(single) + from_next.astype(single)).astype(narrow)
    d_qkv = jnp.concatenate([d_query, d_pairs[0], d_pairs[1]], axis=1)
    totals = jnp.sum(per_shard.astype(single), axis=0)
    own_rows = jnp.concatenate(
        [totals[:part].astype(narrow), in_parts(jnp.sum(totals[part:], axis=0))], axis=0
    )
    whole = lax.all_gather(own_rows, "dp", axis=0).astype(single)
    d_proj = whole[:, :part].reshape(share, width)
    d_gain = jnp.sum(whole[:, part:], axis=(0, 1))
    return (d_stream[None], d_qkv[None], d_proj, d_gain)


def solution(mesh):
    in_specs = (
        P("dp", "cp", None),
        P("dp", "cp"),
        P("dp", None),
        P("dp", "cp", None),
        P(),
        P(None, "cp", "dp"),
        P(None, "dp"),
        P("dp", None),
        P("dp", "cp", None),
        P("cp", None),
    )
    out_specs = (P("dp", "cp", None), P("dp", "cp", None), P("cp", None), P())
    return jax.shard_map(local, mesh=mesh, in_specs=in_specs, out_specs=out_specs, check_vma=False)
```

```python
import math

import jax
import jax.numpy as jnp
from jax import lax
from jax.experimental import pallas as pl
from jax.experimental.pallas import tpu as pltpu
from jax.sharding import PartitionSpec as P

HEADS = 16
HEAD_DIM = 80


EPS = 1e-06


def from_behind(block, axis, distance):
    devices = range(lax.axis_size(axis))
    route = [(i - distance, i) for i in devices if i - distance in devices]
    return lax.ppermute(block, axis, route)


def by_core(block, dim, own):
    core = lax.axis_index("dp") % 2
    return lax.dynamic_index_in_dim(block, core if own else 1 - core, dim, keepdims=False)


def added_on_chip(partial_of):
    count = lax.axis_size("dp")
    swap = [(i, i ^ 1) for i in range(count)]
    received = lax.ppermute(partial_of(False).astype(jnp.bfloat16), "dp", swap)
    return (partial_of(True) + received.astype(jnp.float32)).astype(jnp.bfloat16)


def scattered_over_y(pair):
    count = lax.axis_size("dp")
    groups = [list(range(core, count, 2)) for core in range(2)]
    return lax.psum_scatter(
        pair, "dp", scatter_dimension=0, axis_index_groups=groups, tiled=True
    )


def gelu_slope(pre_value):
    normal_cdf = 0.5 * (1.0 + lax.erf(pre_value * 0.7071067811865476))
    density = jnp.exp(-0.5 * pre_value * pre_value) * 0.3989422804014327
    return normal_cdf + pre_value * density


def in_parts(vector):
    parts = []
    for _ in range(3):
        part = lax.reduce_precision(vector, 8, 7)
        parts.append(part.astype(jnp.bfloat16))
        vector = vector - part
    return jnp.stack(parts)


GROUP = 8
CONTRACT_LAST = (((1,), (1,)), ((), ()))
CONTRACT_FIRST = (((0,), (0,)), ((), ()))
CONTRACT_INNER = (((1,), (0,)), ((), ()))


def mxu(a, b, dims):
    return lax.dot_general(a, b, dims, preferred_element_type=jnp.float32)


def head_columns(ref, head):
    return ref[..., head * HEAD_DIM : (head + 1) * HEAD_DIM]


def window(low_ref, own_ref, high_ref, head):
    parts = [head_columns(low_ref, head), head_columns(own_ref, head)[0]]
    return jnp.concatenate(parts + [head_columns(high_ref, head)], axis=0)


def forward_kernel(q_ref, k_ref, v_ref, kl_ref, vl_ref, kh_ref, vh_ref, rows_ref, keys_ref,
                   att_ref, lse_ref):
    scale = 1.0 / math.sqrt(HEAD_DIM)
    mask = rows_ref[...] == keys_ref[...]
    outs = []
    stats = []
    for head in range(GROUP):
        queries = head_columns(q_ref, head)[0]
        key_heads = window(kl_ref, k_ref, kh_ref, head)
        value_heads = window(vl_ref, v_ref, vh_ref, head)
        scores = jnp.where(mask, mxu(queries, key_heads, CONTRACT_LAST) * scale, -1e30)
        row_max = jnp.max(scores, axis=-1, keepdims=True)
        weights = jnp.exp(scores - row_max)
        total = jnp.sum(weights, axis=-1, keepdims=True)
        probs_low = (weights * (1.0 / total)).astype(jnp.bfloat16)
        outs.append(mxu(probs_low, value_heads, CONTRACT_INNER).astype(jnp.bfloat16))
        stats.append(row_max + jnp.log(total))
    att_ref[...] = jnp.concatenate(outs, axis=1)
    lse_ref[0] = jnp.concatenate(stats, axis=1)


def backward_kernel(q_ref, k_ref, v_ref, kl_ref, vl_ref, kh_ref, vh_ref, rows_ref, keys_ref,
                    att_ref, lse_ref, do_ref,
                    dq_ref, low_ref, own_ref, high_ref):
    scale = 1.0 / math.sqrt(HEAD_DIM)
    narrow = jnp.bfloat16
    patches = dq_ref.shape[0]
    mask = rows_ref[...] == keys_ref[...]
    d_query = []
    d_pairs = ([], [])
    for head in range(GROUP):
        queries = head_columns(q_ref, head)[0]
        key_heads = window(kl_ref, k_ref, kh_ref, head)
        value_heads = window(vl_ref, v_ref, vh_ref, head)
        d_heads = head_columns(do_ref, head)
        scores = jnp.where(mask, mxu(queries, key_heads, CONTRACT_LAST) * scale, -1e30)
        probs = jnp.exp(scores - lse_ref[0, :, head : head + 1])
        probs_low = probs.astype(narrow)
        delta = jnp.sum(
            d_heads.astype(jnp.float32) * head_columns(att_ref, head).astype(jnp.float32),
            axis=-1,
            keepdims=True,
        )
        d_probs = mxu(d_heads, value_heads, CONTRACT_LAST)
        d_scores = (probs * ((d_probs - delta) * scale)).astype(narrow)
        d_query.append(mxu(d_scores, key_heads, CONTRACT_INNER).astype(narrow))
        d_pairs[0].append(mxu(d_scores, queries, CONTRACT_FIRST))
        d_pairs[1].append(mxu(probs_low, d_heads, CONTRACT_FIRST))
    dq_ref[...] = jnp.concatenate(d_query, axis=1)
    for i in range(2):
        total = jnp.concatenate(d_pairs[i], axis=1)
        low_ref[i] = total[:patches].astype(narrow)
        own_ref[i] = total[patches : 2 * patches]
        high_ref[i] = total[2 * patches :].astype(narrow)


def attention_calls(qkv, low, high, seg_rows, seg_keys):
    patches = qkv.shape[1]
    width = qkv.shape[2] // 3
    lanes = GROUP * HEAD_DIM
    groups = width // lanes
    own = [
        pl.BlockSpec((1, patches, lanes), lambda g, i=i: (0, 0, i * groups + g)) for i in range(3)
    ]
    halo = [
        pl.BlockSpec((patches, lanes), lambda g, i=i: (0, i * groups + g)) for i in (0, 1, 0, 1)
    ]
    ids = [
        pl.BlockSpec((patches, 1), lambda g: (0, 0)),
        pl.BlockSpec((1, 3 * patches), lambda g: (0, 0)),
    ]
    operands = (qkv, qkv, qkv, low, low, high, high, seg_rows[:, None], seg_keys[None, :])
    flat = pl.BlockSpec((patches, lanes), lambda g: (0, g))
    stat = pl.BlockSpec((1, patches, GROUP), lambda g: (g, 0, 0))
    pair = pl.BlockSpec((2, patches, lanes), lambda g: (0, 0, g))
    params = pltpu.CompilerParams(vmem_limit_bytes=48 * 1024 * 1024)
    flops = 2 * 3 * patches * patches * width
    exps = 3 * patches * patches * HEADS

    def cost(dots):
        return pl.CostEstimate(
            flops=dots * flops, bytes_accessed=12 * patches * width, transcendentals=exps
        )

    attention, stats = pl.pallas_call(
        forward_kernel,
        grid=(groups,),
        in_specs=own + halo + ids,
        out_specs=(flat, stat),
        out_shape=(
            jax.ShapeDtypeStruct((patches, width), jnp.bfloat16),
            jax.ShapeDtypeStruct((groups, patches, GROUP), jnp.float32),
        ),
        compiler_params=params,
        cost_estimate=cost(2),
        name="attention_forward",
    )(*operands)

    def backward(d_out):
        return pl.pallas_call(
            backward_kernel,
            grid=(groups,),
            in_specs=own + halo + ids + [flat, stat, flat],
            out_specs=(flat, pair, pair, pair),
            out_shape=(
                jax.ShapeDtypeStruct((patches, width), jnp.bfloat16),
                jax.ShapeDtypeStruct((2, patches, width), jnp.bfloat16),
                jax.ShapeDtypeStruct((2, patches, width), jnp.float32),
                jax.ShapeDtypeStruct((2, patches, width), jnp.bfloat16),
            ),
            compiler_params=params,
            cost_estimate=cost(5),
            name="attention_backward",
        )(*operands, attention, stats, d_out)

    return attention, backward


def local(llm_grads, llm_owner, image_ids, stream, ln_gain, pre_act, w_in, w_out, qkv, w_proj):
    single = jnp.float32
    narrow = jnp.bfloat16
    shards = lax.axis_size("cp")
    batches = lax.axis_size("dp")
    device_index = lax.axis_index("cp")
    row_count = llm_grads.shape[1]
    patches = stream.shape[1]
    width = stream.shape[2]
    hidden = w_out.shape[0]
    slot_count = 2 * row_count // shards
    rows = batches * row_count
    packed_width = -(-(hidden + 1) // 128) * 128
    gathered = lax.all_gather(llm_grads[0], "dp", axis=0, tiled=True)
    share = w_proj.shape[0]
    part = share // batches
    own_proj = lax.dynamic_slice_in_dim(w_proj, lax.axis_index("dp") * part, part, 0)
    proj_parts = lax.all_to_all(
        jnp.broadcast_to(own_proj[None], (shards, part, width)),
        "cp",
        split_axis=0,
        concat_axis=0,
        tiled=True,
    ).reshape(shards * part, width)
    proj_parts, key_values, own_owners = lax.optimization_barrier(
        (proj_parts, qkv[0, :, width:], llm_owner[0])
    )
    owners = lax.all_gather(own_owners, "dp", axis=0)
    gathered, proj_parts, owners = lax.optimization_barrier((gathered, proj_parts, owners))
    full_proj = lax.all_gather(proj_parts, "dp", axis=0, tiled=True)
    low = from_behind(key_values, "cp", 1)
    high = from_behind(key_values, "cp", -1)
    target = owners // row_count
    place = (owners % row_count).reshape(rows, 1)
    same_target = target[:, :, None] == target[:, None, :]
    before = jnp.arange(row_count)[None, :] < jnp.arange(row_count)[:, None]
    rank = jnp.sum((same_target & before[None]).astype(jnp.int32), axis=2)
    batch_of = jnp.arange(batches, dtype=jnp.int32)[:, None]
    slot = ((target * batches + batch_of) * slot_count + rank).reshape(1, rows)
    slots = shards * batches * slot_count
    pick = (jnp.arange(slots, dtype=jnp.int32)[:, None] == slot).astype(narrow)
    d_rows = jnp.dot(gathered, w_out.T, preferred_element_type=single).astype(narrow)
    d_rows, low, high = lax.optimization_barrier((d_rows, low, high))
    tags = jnp.where(
        jnp.arange(packed_width - hidden)[None, :] == 0, place + 1, 0
    ).astype(narrow)
    outgoing = jnp.dot(
        pick, jnp.concatenate([d_rows, tags], axis=1), preferred_element_type=single
    ).astype(narrow)
    arrived = lax.all_to_all(
        outgoing.reshape(shards, batches * slot_count, packed_width),
        "cp",
        split_axis=0,
        concat_axis=0,
        tiled=True,
    ).reshape(slots, packed_width)
    arrived, full_proj = lax.optimization_barrier((arrived, full_proj))
    tag_row = arrived[:, hidden].astype(jnp.int32).reshape(1, slots)
    slot_batch = (jnp.arange(slots, dtype=jnp.int32) // slot_count % batches)[None, :]
    home = jnp.where(tag_row > 0, slot_batch * row_count + tag_row - 1, -1)
    settle = (jnp.arange(rows, dtype=jnp.int32)[:, None] == home).astype(narrow)
    d_hidden = jnp.dot(settle, arrived, preferred_element_type=single)[:, :hidden].reshape(
        batches, row_count, hidden
    )
    saved_pre = pre_act.astype(single)
    d_pre = (d_hidden * gelu_slope(saved_pre)).astype(narrow)
    d_norm = added_on_chip(
        lambda own: (
            jnp.einsum(
                "bmh,ih->bmi",
                by_core(d_pre.reshape(batches // 2, 2, row_count, hidden), 1, own),
                w_in,
                preferred_element_type=single,
            )
        )
    )
    d_norm = scattered_over_y(d_norm)
    segment = jnp.repeat(image_ids[0], 4)
    seg_rim = jnp.full((patches,), -1, jnp.int32)
    seg_pad = jnp.concatenate([seg_rim, segment, seg_rim], axis=0)
    seg_keys = lax.dynamic_slice_in_dim(seg_pad, device_index * patches, 3 * patches, 0)
    seg_rows = lax.dynamic_slice_in_dim(segment, device_index * patches, patches, 0)
    attention, backward = attention_calls(qkv, low, high, seg_rows, seg_keys)
    column = jnp.arange(width // 2, dtype=jnp.int32)
    column_base = column // part % shards * share + column // (part * shards) * (2 * part)
    column_base = (column_base + column % part)[None, :]
    feature = jnp.arange(width, dtype=jnp.int32)[:, None]
    core = lax.axis_index("dp") % 2

    def features_of(core):
        pick_columns = (feature == column_base + core * part).astype(narrow)
        return jnp.dot(attention, pick_columns, preferred_element_type=single).astype(narrow)

    other_features, own_features = features_of(1 - core), features_of(core)
    stream_wide = stream[0].astype(single)
    inverse = lax.rsqrt(jnp.mean(stream_wide * stream_wide, axis=-1, keepdims=True) + EPS)
    normed = stream_wide * inverse
    d_norm, other_features, own_features = lax.optimization_barrier(
        (d_norm, other_features, own_features)
    )
    d_norm = lax.optimization_barrier(d_norm.reshape(patches, width)).astype(single)
    gain_part = jnp.sum(d_norm * normed, axis=0)
    d_normed = d_norm * ln_gain
    d_stream = (
        inverse * (d_normed - normed * jnp.mean(d_normed * normed, axis=-1, keepdims=True))
    ).astype(narrow)
    d_stream = lax.optimization_barrier(d_stream)
    d_proj_pair = added_on_chip(
        lambda own: jnp.einsum(
            "pi,pj->ij",
            own_features if own else other_features,
            d_stream,
            preferred_element_type=single,
        )
    )
    d_out = jnp.einsum(
        "pj,ij->pi", d_stream, full_proj, preferred_element_type=single
    ).astype(narrow)
    row = jnp.arange(width, dtype=jnp.int32)
    natural = row // part % shards * share + row // (part * shards) * part + row % part
    order = (natural[:, None] == jnp.arange(width, dtype=jnp.int32)[None, :]).astype(narrow)
    d_out = jnp.dot(d_out, order, preferred_element_type=single).astype(narrow)
    d_proj_pair, d_out = lax.optimization_barrier((d_proj_pair, d_out))
    over_batches = scattered_over_y(d_proj_pair)
    d_query, d_low, d_own, d_high = backward(d_out)
    over_batches, d_query = lax.optimization_barrier((over_batches, d_query))
    from_prev = from_behind(d_high, "cp", 1)
    from_next = from_behind(d_low, "cp", -1)
    spread = jnp.concatenate(
        [
            over_batches.reshape(shards, part, width),
            jnp.broadcast_to(in_parts(gain_part)[None], (shards, 3, width)),
        ],
        axis=1,
    )
    per_shard = lax.all_to_all(spread, "cp", split_axis=0, concat_axis=0, tiled=True)
    per_shard, from_prev, from_next = lax.optimization_barrier((per_shard, from_prev, from_next))
    d_pairs = (d_own + from_prev.astype(single) + from_next.astype(single)).astype(narrow)
    d_qkv = jnp.concatenate([d_query, d_pairs[0], d_pairs[1]], axis=1)
    totals = jnp.sum(per_shard.astype(single), axis=0)
    own_rows = jnp.concatenate(
        [totals[:part].astype(narrow), in_parts(jnp.sum(totals[part:], axis=0))], axis=0
    )
    whole = lax.all_gather(own_rows, "dp", axis=0).astype(single)
    d_proj = whole[:, :part].reshape(share, width)
    d_gain = jnp.sum(whole[:, part:], axis=(0, 1))
    return (d_stream[None], d_qkv[None], d_proj, d_gain)


def solution(mesh):
    in_specs = (
        P("dp", "cp", None),
        P("dp", "cp"),
        P("dp", None),
        P("dp", "cp", None),
        P(),
        P(None, "cp", "dp"),
        P(None, "dp"),
        P("dp", None),
        P("dp", "cp", None),
        P("cp", None),
    )
    out_specs = (P("dp", "cp", None), P("dp", "cp", None), P("cp", None), P())
    return jax.shard_map(local, mesh=mesh, in_specs=in_specs, out_specs=out_specs, check_vma=False)
```

```python
import math

import jax
import jax.numpy as jnp
from jax import lax
from jax.experimental import pallas as pl
from jax.experimental.pallas import tpu as pltpu
from jax.sharding import PartitionSpec as P

HEADS = 16
HEAD_DIM = 80


EPS = 1e-06


def from_behind(block, axis, distance):
    devices = range(lax.axis_size(axis))
    route = [(i - distance, i) for i in devices if i - distance in devices]
    return lax.ppermute(block, axis, route)


def by_core(block, dim, own):
    core = lax.axis_index("dp") % 2
    return lax.dynamic_index_in_dim(block, core if own else 1 - core, dim, keepdims=False)


def added_on_chip(partial_of):
    count = lax.axis_size("dp")
    swap = [(i, i ^ 1) for i in range(count)]
    received = lax.ppermute(partial_of(False).astype(jnp.bfloat16), "dp", swap)
    return (partial_of(True) + received.astype(jnp.float32)).astype(jnp.bfloat16)


def scattered_over_y(pair):
    count = lax.axis_size("dp")
    groups = [list(range(core, count, 2)) for core in range(2)]
    return lax.psum_scatter(
        pair, "dp", scatter_dimension=0, axis_index_groups=groups, tiled=True
    )


def gelu_slope(pre_value):
    normal_cdf = 0.5 * (1.0 + lax.erf(pre_value * 0.7071067811865476))
    density = jnp.exp(-0.5 * pre_value * pre_value) * 0.3989422804014327
    return normal_cdf + pre_value * density


def in_parts(vector):
    parts = []
    for _ in range(3):
        part = lax.reduce_precision(vector, 8, 7)
        parts.append(part.astype(jnp.bfloat16))
        vector = vector - part
    return jnp.stack(parts)


GROUP = 8
CONTRACT_LAST = (((1,), (1,)), ((), ()))
CONTRACT_FIRST = (((0,), (0,)), ((), ()))
CONTRACT_INNER = (((1,), (0,)), ((), ()))


def mxu(a, b, dims):
    return lax.dot_general(a, b, dims, preferred_element_type=jnp.float32)


def head_columns(ref, head):
    return ref[..., head * HEAD_DIM : (head + 1) * HEAD_DIM]


def window(low_ref, own_ref, high_ref, head):
    parts = [head_columns(low_ref, head), head_columns(own_ref, head)[0]]
    return jnp.concatenate(parts + [head_columns(high_ref, head)], axis=0)


def forward_kernel(q_ref, k_ref, v_ref, kl_ref, vl_ref, kh_ref, vh_ref, rows_ref, keys_ref,
                   att_ref, lse_ref):
    scale = 1.0 / math.sqrt(HEAD_DIM)
    mask = rows_ref[...] == keys_ref[...]
    outs = []
    stats = []
    for head in range(GROUP):
        queries = head_columns(q_ref, head)[0]
        key_heads = window(kl_ref, k_ref, kh_ref, head)
        value_heads = window(vl_ref, v_ref, vh_ref, head)
        scores = jnp.where(mask, mxu(queries, key_heads, CONTRACT_LAST) * scale, -1e30)
        row_max = jnp.max(scores, axis=-1, keepdims=True)
        weights = jnp.exp(scores - row_max)
        total = jnp.sum(weights, axis=-1, keepdims=True)
        probs_low = (weights * (1.0 / total)).astype(jnp.bfloat16)
        outs.append(mxu(probs_low, value_heads, CONTRACT_INNER).astype(jnp.bfloat16))
        stats.append(row_max + jnp.log(total))
    att_ref[...] = jnp.concatenate(outs, axis=1)
    lse_ref[0] = jnp.concatenate(stats, axis=1)


def backward_kernel(q_ref, k_ref, v_ref, kl_ref, vl_ref, kh_ref, vh_ref, rows_ref, keys_ref,
                    att_ref, lse_ref, do_ref,
                    dq_ref, low_ref, own_ref, high_ref):
    scale = 1.0 / math.sqrt(HEAD_DIM)
    narrow = jnp.bfloat16
    patches = dq_ref.shape[0]
    mask = rows_ref[...] == keys_ref[...]
    d_query = []
    d_pairs = ([], [])
    for head in range(GROUP):
        queries = head_columns(q_ref, head)[0]
        key_heads = window(kl_ref, k_ref, kh_ref, head)
        value_heads = window(vl_ref, v_ref, vh_ref, head)
        d_heads = head_columns(do_ref, head)
        scores = jnp.where(mask, mxu(queries, key_heads, CONTRACT_LAST) * scale, -1e30)
        probs = jnp.exp(scores - lse_ref[0, :, head : head + 1])
        probs_low = probs.astype(narrow)
        delta = jnp.sum(
            d_heads.astype(jnp.float32) * head_columns(att_ref, head).astype(jnp.float32),
            axis=-1,
            keepdims=True,
        )
        d_probs = mxu(d_heads, value_heads, CONTRACT_LAST)
        d_scores = (probs * ((d_probs - delta) * scale)).astype(narrow)
        d_query.append(mxu(d_scores, key_heads, CONTRACT_INNER).astype(narrow))
        d_pairs[0].append(mxu(d_scores, queries, CONTRACT_FIRST))
        d_pairs[1].append(mxu(probs_low, d_heads, CONTRACT_FIRST))
    dq_ref[...] = jnp.concatenate(d_query, axis=1)
    for i in range(2):
        total = jnp.concatenate(d_pairs[i], axis=1)
        low_ref[i] = total[:patches].astype(narrow)
        own_ref[i] = total[patches : 2 * patches]
        high_ref[i] = total[2 * patches :].astype(narrow)


def attention_calls(qkv, low, high, seg_rows, seg_keys):
    patches = qkv.shape[1]
    width = qkv.shape[2] // 3
    lanes = GROUP * HEAD_DIM
    groups = width // lanes
    own = [
        pl.BlockSpec((1, patches, lanes), lambda g, i=i: (0, 0, i * groups + g)) for i in range(3)
    ]
    halo = [
        pl.BlockSpec((patches, lanes), lambda g, i=i: (0, i * groups + g)) for i in (0, 1, 0, 1)
    ]
    ids = [
        pl.BlockSpec((patches, 1), lambda g: (0, 0)),
        pl.BlockSpec((1, 3 * patches), lambda g: (0, 0)),
    ]
    operands = (qkv, qkv, qkv, low, low, high, high, seg_rows[:, None], seg_keys[None, :])
    flat = pl.BlockSpec((patches, lanes), lambda g: (0, g))
    stat = pl.BlockSpec((1, patches, GROUP), lambda g: (g, 0, 0))
    pair = pl.BlockSpec((2, patches, lanes), lambda g: (0, 0, g))
    params = pltpu.CompilerParams(vmem_limit_bytes=48 * 1024 * 1024)
    flops = 2 * 3 * patches * patches * width
    exps = 3 * patches * patches * HEADS

    def cost(dots):
        return pl.CostEstimate(
            flops=dots * flops, bytes_accessed=12 * patches * width, transcendentals=exps
        )

    attention, stats = pl.pallas_call(
        forward_kernel,
        grid=(groups,),
        in_specs=own + halo + ids,
        out_specs=(flat, stat),
        out_shape=(
            jax.ShapeDtypeStruct((patches, width), jnp.bfloat16),
            jax.ShapeDtypeStruct((groups, patches, GROUP), jnp.float32),
        ),
        compiler_params=params,
        cost_estimate=cost(2),
        name="attention_forward",
    )(*operands)

    def backward(d_out):
        return pl.pallas_call(
            backward_kernel,
            grid=(groups,),
            in_specs=own + halo + ids + [flat, stat, flat],
            out_specs=(flat, pair, pair, pair),
            out_shape=(
                jax.ShapeDtypeStruct((patches, width), jnp.bfloat16),
                jax.ShapeDtypeStruct((2, patches, width), jnp.bfloat16),
                jax.ShapeDtypeStruct((2, patches, width), jnp.float32),
                jax.ShapeDtypeStruct((2, patches, width), jnp.bfloat16),
            ),
            compiler_params=params,
            cost_estimate=cost(5),
            name="attention_backward",
        )(*operands, attention, stats, d_out)

    return attention, backward


def local(llm_grads, llm_owner, image_ids, stream, ln_gain, pre_act, w_in, w_out, qkv, w_proj):
    single = jnp.float32
    narrow = jnp.bfloat16
    shards = lax.axis_size("cp")
    batches = lax.axis_size("dp")
    device_index = lax.axis_index("cp")
    row_count = llm_grads.shape[1]
    patches = stream.shape[1]
    width = stream.shape[2]
    hidden = w_out.shape[0]
    slot_count = 2 * row_count // shards
    rows = batches * row_count
    packed_width = -(-(hidden + 1) // 128) * 128
    gathered = lax.all_gather(llm_grads[0], "dp", axis=0, tiled=True)
    share = w_proj.shape[0]
    part = share // batches
    own_proj = lax.dynamic_slice_in_dim(w_proj, lax.axis_index("dp") * part, part, 0)
    proj_parts = lax.all_to_all(
        jnp.broadcast_to(own_proj[None], (shards, part, width)),
        "cp",
        split_axis=0,
        concat_axis=0,
        tiled=True,
    ).reshape(shards * part, width)
    proj_parts, key_values, own_owners = lax.optimization_barrier(
        (proj_parts, qkv[0, :, width:], llm_owner[0])
    )
    owners = lax.all_gather(own_owners, "dp", axis=0)
    gathered, proj_parts, owners = lax.optimization_barrier((gathered, proj_parts, owners))
    full_proj = lax.all_gather(proj_parts, "dp", axis=0, tiled=True)
    low = from_behind(key_values, "cp", 1)
    high = from_behind(key_values, "cp", -1)
    target = owners // row_count
    place = (owners % row_count).reshape(rows, 1)
    same_target = target[:, :, None] == target[:, None, :]
    before = jnp.arange(row_count)[None, :] < jnp.arange(row_count)[:, None]
    rank = jnp.sum((same_target & before[None]).astype(jnp.int32), axis=2)
    batch_of = jnp.arange(batches, dtype=jnp.int32)[:, None]
    slot = ((target * batches + batch_of) * slot_count + rank).reshape(1, rows)
    slots = shards * batches * slot_count
    pick = (jnp.arange(slots, dtype=jnp.int32)[:, None] == slot).astype(narrow)
    d_rows = jnp.dot(gathered, w_out.T, preferred_element_type=single).astype(narrow)
    tags = jnp.where(
        jnp.arange(packed_width - hidden)[None, :] == 0, place + 1, 0
    ).astype(narrow)
    outgoing = jnp.dot(
        pick, jnp.concatenate([d_rows, tags], axis=1), preferred_element_type=single
    ).astype(narrow)
    arrived = lax.all_to_all(
        outgoing.reshape(shards, batches * slot_count, packed_width),
        "cp",
        split_axis=0,
        concat_axis=0,
        tiled=True,
    ).reshape(slots, packed_width)
    arrived, full_proj, low, high = lax.optimization_barrier((arrived, full_proj, low, high))
    tag_row = arrived[:, hidden].astype(jnp.int32).reshape(1, slots)
    slot_batch = (jnp.arange(slots, dtype=jnp.int32) // slot_count % batches)[None, :]
    home = jnp.where(tag_row > 0, slot_batch * row_count + tag_row - 1, -1)
    settle = (jnp.arange(rows, dtype=jnp.int32)[:, None] == home).astype(narrow)
    d_hidden = jnp.dot(settle, arrived, preferred_element_type=single)[:, :hidden].reshape(
        batches, row_count, hidden
    )
    saved_pre = pre_act.astype(single)
    d_pre = (d_hidden * gelu_slope(saved_pre)).astype(narrow)
    d_norm = added_on_chip(
        lambda own: (
            jnp.einsum(
                "bmh,ih->bmi",
                by_core(d_pre.reshape(batches // 2, 2, row_count, hidden), 1, own),
                w_in,
                preferred_element_type=single,
            )
        )
    )
    d_norm = scattered_over_y(d_norm)
    segment = jnp.repeat(image_ids[0], 4)
    seg_rim = jnp.full((patches,), -1, jnp.int32)
    seg_pad = jnp.concatenate([seg_rim, segment, seg_rim], axis=0)
    seg_keys = lax.dynamic_slice_in_dim(seg_pad, device_index * patches, 3 * patches, 0)
    seg_rows = lax.dynamic_slice_in_dim(segment, device_index * patches, patches, 0)
    attention, backward = attention_calls(qkv, low, high, seg_rows, seg_keys)
    column = jnp.arange(width // 2, dtype=jnp.int32)
    column_base = column // part % shards * share + column // (part * shards) * (2 * part)
    column_base = (column_base + column % part)[None, :]
    feature = jnp.arange(width, dtype=jnp.int32)[:, None]
    core = lax.axis_index("dp") % 2

    def features_of(core):
        pick_columns = (feature == column_base + core * part).astype(narrow)
        return jnp.dot(attention, pick_columns, preferred_element_type=single).astype(narrow)

    other_features, own_features = features_of(1 - core), features_of(core)
    stream_wide = stream[0].astype(single)
    inverse = lax.rsqrt(jnp.mean(stream_wide * stream_wide, axis=-1, keepdims=True) + EPS)
    normed = stream_wide * inverse
    d_norm, other_features, own_features = lax.optimization_barrier(
        (d_norm, other_features, own_features)
    )
    d_norm = lax.optimization_barrier(d_norm.reshape(patches, width)).astype(single)
    gain_part = jnp.sum(d_norm * normed, axis=0)
    d_normed = d_norm * ln_gain
    d_stream = (
        inverse * (d_normed - normed * jnp.mean(d_normed * normed, axis=-1, keepdims=True))
    ).astype(narrow)
    d_stream = lax.optimization_barrier(d_stream)
    d_proj_pair = added_on_chip(
        lambda own: jnp.einsum(
            "pi,pj->ij",
            own_features if own else other_features,
            d_stream,
            preferred_element_type=single,
        )
    )
    d_out = jnp.einsum(
        "pj,ij->pi", d_stream, full_proj, preferred_element_type=single
    ).astype(narrow)
    row = jnp.arange(width, dtype=jnp.int32)
    natural = row // part % shards * share + row // (part * shards) * part + row % part
    order = (natural[:, None] == jnp.arange(width, dtype=jnp.int32)[None, :]).astype(narrow)
    d_out = jnp.dot(d_out, order, preferred_element_type=single).astype(narrow)
    d_proj_pair, d_out = lax.optimization_barrier((d_proj_pair, d_out))
    over_batches = scattered_over_y(d_proj_pair)
    d_query, d_low, d_own, d_high = backward(d_out)
    over_batches, d_query = lax.optimization_barrier((over_batches, d_query))
    from_prev = from_behind(d_high, "cp", 1)
    from_next = from_behind(d_low, "cp", -1)
    spread = jnp.concatenate(
        [
            over_batches.reshape(shards, part, width),
            jnp.broadcast_to(in_parts(gain_part)[None], (shards, 3, width)),
        ],
        axis=1,
    )
    per_shard = lax.all_to_all(spread, "cp", split_axis=0, concat_axis=0, tiled=True)
    d_pairs = (d_own + from_prev.astype(single) + from_next.astype(single)).astype(narrow)
    d_qkv = jnp.concatenate([d_query, d_pairs[0], d_pairs[1]], axis=1)
    totals = jnp.sum(per_shard.astype(single), axis=0)
    own_rows = jnp.concatenate(
        [totals[:part].astype(narrow), in_parts(jnp.sum(totals[part:], axis=0))], axis=0
    )
    whole = lax.all_gather(own_rows, "dp", axis=0).astype(single)
    d_proj = whole[:, :part].reshape(share, width)
    d_gain = jnp.sum(whole[:, part:], axis=(0, 1))
    return (d_stream[None], d_qkv[None], d_proj, d_gain)


def solution(mesh):
    in_specs = (
        P("dp", "cp", None),
        P("dp", "cp"),
        P("dp", None),
        P("dp", "cp", None),
        P(),
        P(None, "cp", "dp"),
        P(None, "dp"),
        P("dp", None),
        P("dp", "cp", None),
        P("cp", None),
    )
    out_specs = (P("dp", "cp", None), P("dp", "cp", None), P("cp", None), P())
    return jax.shard_map(local, mesh=mesh, in_specs=in_specs, out_specs=out_specs, check_vma=False)
```

```python
import math

import jax
import jax.numpy as jnp
from jax import lax
from jax.experimental import pallas as pl
from jax.experimental.pallas import tpu as pltpu
from jax.sharding import PartitionSpec as P

HEADS = 16
HEAD_DIM = 80


EPS = 1e-06


def from_behind(block, axis, distance):
    devices = range(lax.axis_size(axis))
    route = [(i - distance, i) for i in devices if i - distance in devices]
    return lax.ppermute(block, axis, route)


def by_core(block, dim, own):
    core = lax.axis_index("dp") % 2
    return lax.dynamic_index_in_dim(block, core if own else 1 - core, dim, keepdims=False)


def added_on_chip(partial_of):
    count = lax.axis_size("dp")
    swap = [(i, i ^ 1) for i in range(count)]
    received = lax.ppermute(partial_of(False).astype(jnp.bfloat16), "dp", swap)
    return (partial_of(True) + received.astype(jnp.float32)).astype(jnp.bfloat16)


def scattered_over_y(pair):
    count = lax.axis_size("dp")
    groups = [list(range(core, count, 2)) for core in range(2)]
    return lax.psum_scatter(
        pair, "dp", scatter_dimension=0, axis_index_groups=groups, tiled=True
    )


def gelu_slope(pre_value):
    normal_cdf = 0.5 * (1.0 + lax.erf(pre_value * 0.7071067811865476))
    density = jnp.exp(-0.5 * pre_value * pre_value) * 0.3989422804014327
    return normal_cdf + pre_value * density


def in_parts(vector):
    parts = []
    for _ in range(3):
        part = lax.reduce_precision(vector, 8, 7)
        parts.append(part.astype(jnp.bfloat16))
        vector = vector - part
    return jnp.stack(parts)


GROUP = 8
CONTRACT_LAST = (((1,), (1,)), ((), ()))
CONTRACT_FIRST = (((0,), (0,)), ((), ()))
CONTRACT_INNER = (((1,), (0,)), ((), ()))


def mxu(a, b, dims):
    return lax.dot_general(a, b, dims, preferred_element_type=jnp.float32)


def head_columns(ref, head):
    return ref[..., head * HEAD_DIM : (head + 1) * HEAD_DIM]


def window(low_ref, own_ref, high_ref, head):
    parts = [head_columns(low_ref, head), head_columns(own_ref, head)[0]]
    return jnp.concatenate(parts + [head_columns(high_ref, head)], axis=0)


def forward_kernel(q_ref, k_ref, v_ref, kl_ref, vl_ref, kh_ref, vh_ref, rows_ref, keys_ref,
                   att_ref, lse_ref):
    scale = 1.0 / math.sqrt(HEAD_DIM)
    mask = rows_ref[...] == keys_ref[...]
    outs = []
    stats = []
    for head in range(GROUP):
        queries = head_columns(q_ref, head)[0]
        key_heads = window(kl_ref, k_ref, kh_ref, head)
        value_heads = window(vl_ref, v_ref, vh_ref, head)
        scores = jnp.where(mask, mxu(queries, key_heads, CONTRACT_LAST) * scale, -1e30)
        row_max = jnp.max(scores, axis=-1, keepdims=True)
        weights = jnp.exp(scores - row_max)
        total = jnp.sum(weights, axis=-1, keepdims=True)
        probs_low = (weights * (1.0 / total)).astype(jnp.bfloat16)
        outs.append(mxu(probs_low, value_heads, CONTRACT_INNER).astype(jnp.bfloat16))
        stats.append(row_max + jnp.log(total))
    att_ref[...] = jnp.concatenate(outs, axis=1)
    lse_ref[0] = jnp.concatenate(stats, axis=1)


def backward_kernel(q_ref, k_ref, v_ref, kl_ref, vl_ref, kh_ref, vh_ref, rows_ref, keys_ref,
                    att_ref, lse_ref, do_ref,
                    dq_ref, low_ref, own_ref, high_ref):
    scale = 1.0 / math.sqrt(HEAD_DIM)
    narrow = jnp.bfloat16
    patches = dq_ref.shape[0]
    mask = rows_ref[...] == keys_ref[...]
    d_query = []
    d_pairs = ([], [])
    for head in range(GROUP):
        queries = head_columns(q_ref, head)[0]
        key_heads = window(kl_ref, k_ref, kh_ref, head)
        value_heads = window(vl_ref, v_ref, vh_ref, head)
        d_heads = head_columns(do_ref, head)
        scores = jnp.where(mask, mxu(queries, key_heads, CONTRACT_LAST) * scale, -1e30)
        probs = jnp.exp(scores - lse_ref[0, :, head : head + 1])
        probs_low = probs.astype(narrow)
        delta = jnp.sum(
            d_heads.astype(jnp.float32) * head_columns(att_ref, head).astype(jnp.float32),
            axis=-1,
            keepdims=True,
        )
        d_probs = mxu(d_heads, value_heads, CONTRACT_LAST)
        d_scores = (probs * ((d_probs - delta) * scale)).astype(narrow)
        d_query.append(mxu(d_scores, key_heads, CONTRACT_INNER).astype(narrow))
        d_pairs[0].append(mxu(d_scores, queries, CONTRACT_FIRST))
        d_pairs[1].append(mxu(probs_low, d_heads, CONTRACT_FIRST))
    dq_ref[...] = jnp.concatenate(d_query, axis=1)
    for i in range(2):
        total = jnp.concatenate(d_pairs[i], axis=1)
        low_ref[i] = total[:patches].astype(narrow)
        own_ref[i] = total[patches : 2 * patches]
        high_ref[i] = total[2 * patches :].astype(narrow)


def attention_calls(qkv, low, high, seg_rows, seg_keys):
    patches = qkv.shape[1]
    width = qkv.shape[2] // 3
    lanes = GROUP * HEAD_DIM
    groups = width // lanes
    own = [
        pl.BlockSpec((1, patches, lanes), lambda g, i=i: (0, 0, i * groups + g)) for i in range(3)
    ]
    halo = [
        pl.BlockSpec((patches, lanes), lambda g, i=i: (0, i * groups + g)) for i in (0, 1, 0, 1)
    ]
    ids = [
        pl.BlockSpec((patches, 1), lambda g: (0, 0)),
        pl.BlockSpec((1, 3 * patches), lambda g: (0, 0)),
    ]
    operands = (qkv, qkv, qkv, low, low, high, high, seg_rows[:, None], seg_keys[None, :])
    flat = pl.BlockSpec((patches, lanes), lambda g: (0, g))
    stat = pl.BlockSpec((1, patches, GROUP), lambda g: (g, 0, 0))
    pair = pl.BlockSpec((2, patches, lanes), lambda g: (0, 0, g))
    params = pltpu.CompilerParams(vmem_limit_bytes=48 * 1024 * 1024)
    flops = 2 * 3 * patches * patches * width
    exps = 3 * patches * patches * HEADS

    def cost(dots):
        return pl.CostEstimate(
            flops=dots * flops, bytes_accessed=12 * patches * width, transcendentals=exps
        )

    attention, stats = pl.pallas_call(
        forward_kernel,
        grid=(groups,),
        in_specs=own + halo + ids,
        out_specs=(flat, stat),
        out_shape=(
            jax.ShapeDtypeStruct((patches, width), jnp.bfloat16),
            jax.ShapeDtypeStruct((groups, patches, GROUP), jnp.float32),
        ),
        compiler_params=params,
        cost_estimate=cost(2),
        name="attention_forward",
    )(*operands)

    def backward(d_out):
        return pl.pallas_call(
            backward_kernel,
            grid=(groups,),
            in_specs=own + halo + ids + [flat, stat, flat],
            out_specs=(flat, pair, pair, pair),
            out_shape=(
                jax.ShapeDtypeStruct((patches, width), jnp.bfloat16),
                jax.ShapeDtypeStruct((2, patches, width), jnp.bfloat16),
                jax.ShapeDtypeStruct((2, patches, width), jnp.float32),
                jax.ShapeDtypeStruct((2, patches, width), jnp.bfloat16),
            ),
            compiler_params=params,
            cost_estimate=cost(5),
            name="attention_backward",
        )(*operands, attention, stats, d_out)

    return attention, backward


def local(llm_grads, llm_owner, image_ids, stream, ln_gain, pre_act, w_in, w_out, qkv, w_proj):
    single = jnp.float32
    narrow = jnp.bfloat16
    shards = lax.axis_size("cp")
    batches = lax.axis_size("dp")
    device_index = lax.axis_index("cp")
    row_count = llm_grads.shape[1]
    patches = stream.shape[1]
    width = stream.shape[2]
    hidden = w_out.shape[0]
    slot_count = 2 * row_count // shards
    rows = batches * row_count
    packed_width = -(-(hidden + 1) // 128) * 128
    half = llm_grads.shape[2] // 2
    left = lax.all_gather(llm_grads[0, :, :half], "dp", axis=0, tiled=True)
    right = lax.all_gather(llm_grads[0, :, half:], "dp", axis=0, tiled=True)
    share = w_proj.shape[0]
    part = share // batches
    own_proj = lax.dynamic_slice_in_dim(w_proj, lax.axis_index("dp") * part, part, 0)
    proj_parts = lax.all_to_all(
        jnp.broadcast_to(own_proj[None], (shards, part, width)),
        "cp",
        split_axis=0,
        concat_axis=0,
        tiled=True,
    ).reshape(shards * part, width)
    proj_parts, key_values, own_owners = lax.optimization_barrier(
        (proj_parts, qkv[0, :, width:], llm_owner[0])
    )
    owners = lax.all_gather(own_owners, "dp", axis=0)
    right, proj_parts, owners = lax.optimization_barrier((right, proj_parts, owners))
    full_proj = lax.all_gather(proj_parts, "dp", axis=0, tiled=True)
    low = from_behind(key_values, "cp", 1)
    high = from_behind(key_values, "cp", -1)
    target = owners // row_count
    place = (owners % row_count).reshape(rows, 1)
    same_target = target[:, :, None] == target[:, None, :]
    before = jnp.arange(row_count)[None, :] < jnp.arange(row_count)[:, None]
    rank = jnp.sum((same_target & before[None]).astype(jnp.int32), axis=2)
    batch_of = jnp.arange(batches, dtype=jnp.int32)[:, None]
    slot = ((target * batches + batch_of) * slot_count + rank).reshape(1, rows)
    slots = shards * batches * slot_count
    pick = (jnp.arange(slots, dtype=jnp.int32)[:, None] == slot).astype(narrow)
    left_rows = jnp.dot(left, w_out[:, :half].T, preferred_element_type=single)
    right_rows = jnp.dot(right, w_out[:, half:].T, preferred_element_type=single)
    d_rows = (left_rows + right_rows).astype(narrow)
    tags = jnp.where(
        jnp.arange(packed_width - hidden)[None, :] == 0, place + 1, 0
    ).astype(narrow)
    outgoing = jnp.dot(
        pick, jnp.concatenate([d_rows, tags], axis=1), preferred_element_type=single
    ).astype(narrow)
    arrived = lax.all_to_all(
        outgoing.reshape(shards, batches * slot_count, packed_width),
        "cp",
        split_axis=0,
        concat_axis=0,
        tiled=True,
    ).reshape(slots, packed_width)
    arrived, full_proj, low, high = lax.optimization_barrier((arrived, full_proj, low, high))
    tag_row = arrived[:, hidden].astype(jnp.int32).reshape(1, slots)
    slot_batch = (jnp.arange(slots, dtype=jnp.int32) // slot_count % batches)[None, :]
    home = jnp.where(tag_row > 0, slot_batch * row_count + tag_row - 1, -1)
    settle = (jnp.arange(rows, dtype=jnp.int32)[:, None] == home).astype(narrow)
    d_hidden = jnp.dot(settle, arrived, preferred_element_type=single)[:, :hidden].reshape(
        batches, row_count, hidden
    )
    saved_pre = pre_act.astype(single)
    d_pre = (d_hidden * gelu_slope(saved_pre)).astype(narrow)
    d_norm = added_on_chip(
        lambda own: (
            jnp.einsum(
                "bmh,ih->bmi",
                by_core(d_pre.reshape(batches // 2, 2, row_count, hidden), 1, own),
                w_in,
                preferred_element_type=single,
            )
        )
    )
    d_norm = scattered_over_y(d_norm)
    segment = jnp.repeat(image_ids[0], 4)
    seg_rim = jnp.full((patches,), -1, jnp.int32)
    seg_pad = jnp.concatenate([seg_rim, segment, seg_rim], axis=0)
    seg_keys = lax.dynamic_slice_in_dim(seg_pad, device_index * patches, 3 * patches, 0)
    seg_rows = lax.dynamic_slice_in_dim(segment, device_index * patches, patches, 0)
    attention, backward = attention_calls(qkv, low, high, seg_rows, seg_keys)
    column = jnp.arange(width // 2, dtype=jnp.int32)
    column_base = column // part % shards * share + column // (part * shards) * (2 * part)
    column_base = (column_base + column % part)[None, :]
    feature = jnp.arange(width, dtype=jnp.int32)[:, None]
    core = lax.axis_index("dp") % 2

    def features_of(core):
        pick_columns = (feature == column_base + core * part).astype(narrow)
        return jnp.dot(attention, pick_columns, preferred_element_type=single).astype(narrow)

    other_features, own_features = features_of(1 - core), features_of(core)
    stream_wide = stream[0].astype(single)
    inverse = lax.rsqrt(jnp.mean(stream_wide * stream_wide, axis=-1, keepdims=True) + EPS)
    normed = stream_wide * inverse
    d_norm, other_features, own_features = lax.optimization_barrier(
        (d_norm, other_features, own_features)
    )
    d_norm = lax.optimization_barrier(d_norm.reshape(patches, width)).astype(single)
    gain_part = jnp.sum(d_norm * normed, axis=0)
    d_normed = d_norm * ln_gain
    d_stream = (
        inverse * (d_normed - normed * jnp.mean(d_normed * normed, axis=-1, keepdims=True))
    ).astype(narrow)
    d_stream = lax.optimization_barrier(d_stream)
    d_proj_pair = added_on_chip(
        lambda own: jnp.einsum(
            "pi,pj->ij",
            own_features if own else other_features,
            d_stream,
            preferred_element_type=single,
        )
    )
    d_out = jnp.einsum(
        "pj,ij->pi", d_stream, full_proj, preferred_element_type=single
    ).astype(narrow)
    row = jnp.arange(width, dtype=jnp.int32)
    natural = row // part % shards * share + row // (part * shards) * part + row % part
    order = (natural[:, None] == jnp.arange(width, dtype=jnp.int32)[None, :]).astype(narrow)
    d_out = jnp.dot(d_out, order, preferred_element_type=single).astype(narrow)
    d_proj_pair, d_out = lax.optimization_barrier((d_proj_pair, d_out))
    over_batches = scattered_over_y(d_proj_pair)
    d_query, d_low, d_own, d_high = backward(d_out)
    over_batches, d_query = lax.optimization_barrier((over_batches, d_query))
    from_prev = from_behind(d_high, "cp", 1)
    from_next = from_behind(d_low, "cp", -1)
    spread = jnp.concatenate(
        [
            over_batches.reshape(shards, part, width),
            jnp.broadcast_to(in_parts(gain_part)[None], (shards, 3, width)),
        ],
        axis=1,
    )
    per_shard = lax.all_to_all(spread, "cp", split_axis=0, concat_axis=0, tiled=True)
    d_pairs = (d_own + from_prev.astype(single) + from_next.astype(single)).astype(narrow)
    d_qkv = jnp.concatenate([d_query, d_pairs[0], d_pairs[1]], axis=1)
    totals = jnp.sum(per_shard.astype(single), axis=0)
    own_rows = jnp.concatenate(
        [totals[:part].astype(narrow), in_parts(jnp.sum(totals[part:], axis=0))], axis=0
    )
    whole = lax.all_gather(own_rows, "dp", axis=0).astype(single)
    d_proj = whole[:, :part].reshape(share, width)
    d_gain = jnp.sum(whole[:, part:], axis=(0, 1))
    return (d_stream[None], d_qkv[None], d_proj, d_gain)


def solution(mesh):
    in_specs = (
        P("dp", "cp", None),
        P("dp", "cp"),
        P("dp", None),
        P("dp", "cp", None),
        P(),
        P(None, "cp", "dp"),
        P(None, "dp"),
        P("dp", None),
        P("dp", "cp", None),
        P("cp", None),
    )
    out_specs = (P("dp", "cp", None), P("dp", "cp", None), P("cp", None), P())
    return jax.shard_map(local, mesh=mesh, in_specs=in_specs, out_specs=out_specs, check_vma=False)
```

```python
import math

import jax
import jax.numpy as jnp
from jax import lax
from jax.experimental import pallas as pl
from jax.experimental.pallas import tpu as pltpu
from jax.sharding import PartitionSpec as P

HEADS = 16
HEAD_DIM = 80


EPS = 1e-06


def from_behind(block, axis, distance):
    devices = range(lax.axis_size(axis))
    route = [(i - distance, i) for i in devices if i - distance in devices]
    return lax.ppermute(block, axis, route)


def by_core(block, dim, own):
    core = lax.axis_index("dp") % 2
    return lax.dynamic_index_in_dim(block, core if own else 1 - core, dim, keepdims=False)


def from_sibling(block):
    return lax.ppermute(block, "dp", [(i, i ^ 1) for i in range(lax.axis_size("dp"))])


def scattered_over_y(pair):
    count = lax.axis_size("dp")
    groups = [list(range(core, count, 2)) for core in range(2)]
    return lax.psum_scatter(
        pair, "dp", scatter_dimension=0, axis_index_groups=groups, tiled=True
    )


def gelu_slope(pre_value):
    normal_cdf = 0.5 * (1.0 + lax.erf(pre_value * 0.7071067811865476))
    density = jnp.exp(-0.5 * pre_value * pre_value) * 0.3989422804014327
    return normal_cdf + pre_value * density


def in_parts(vector):
    parts = []
    for _ in range(3):
        part = lax.reduce_precision(vector, 8, 7)
        parts.append(part.astype(jnp.bfloat16))
        vector = vector - part
    return jnp.stack(parts)


GROUP = 8
CONTRACT_LAST = (((1,), (1,)), ((), ()))
CONTRACT_FIRST = (((0,), (0,)), ((), ()))
CONTRACT_INNER = (((1,), (0,)), ((), ()))


def mxu(a, b, dims):
    return lax.dot_general(a, b, dims, preferred_element_type=jnp.float32)


def head_columns(ref, head):
    return ref[..., head * HEAD_DIM : (head + 1) * HEAD_DIM]


def window(low_ref, own_ref, high_ref, head):
    parts = [head_columns(low_ref, head), head_columns(own_ref, head)[0]]
    return jnp.concatenate(parts + [head_columns(high_ref, head)], axis=0)


def forward_kernel(q_ref, k_ref, v_ref, kl_ref, vl_ref, kh_ref, vh_ref, rows_ref, keys_ref,
                   att_ref, lse_ref):
    scale = 1.0 / math.sqrt(HEAD_DIM)
    mask = rows_ref[...] == keys_ref[...]
    outs = []
    stats = []
    for head in range(GROUP):
        queries = head_columns(q_ref, head)[0]
        key_heads = window(kl_ref, k_ref, kh_ref, head)
        value_heads = window(vl_ref, v_ref, vh_ref, head)
        scores = jnp.where(mask, mxu(queries, key_heads, CONTRACT_LAST) * scale, -1e30)
        row_max = jnp.max(scores, axis=-1, keepdims=True)
        weights = jnp.exp(scores - row_max)
        total = jnp.sum(weights, axis=-1, keepdims=True)
        probs_low = (weights * (1.0 / total)).astype(jnp.bfloat16)
        outs.append(mxu(probs_low, value_heads, CONTRACT_INNER).astype(jnp.bfloat16))
        stats.append(row_max + jnp.log(total))
    att_ref[...] = jnp.concatenate(outs, axis=1)
    lse_ref[0] = jnp.concatenate(stats, axis=1)


def backward_kernel(q_ref, k_ref, v_ref, kl_ref, vl_ref, kh_ref, vh_ref, rows_ref, keys_ref,
                    att_ref, lse_ref, do_ref,
                    dq_ref, low_ref, own_ref, high_ref):
    scale = 1.0 / math.sqrt(HEAD_DIM)
    narrow = jnp.bfloat16
    patches = dq_ref.shape[0]
    mask = rows_ref[...] == keys_ref[...]
    d_query = []
    d_pairs = ([], [])
    for head in range(GROUP):
        queries = head_columns(q_ref, head)[0]
        key_heads = window(kl_ref, k_ref, kh_ref, head)
        value_heads = window(vl_ref, v_ref, vh_ref, head)
        d_heads = head_columns(do_ref, head)
        scores = jnp.where(mask, mxu(queries, key_heads, CONTRACT_LAST) * scale, -1e30)
        probs = jnp.exp(scores - lse_ref[0, :, head : head + 1])
        probs_low = probs.astype(narrow)
        delta = jnp.sum(
            d_heads.astype(jnp.float32) * head_columns(att_ref, head).astype(jnp.float32),
            axis=-1,
            keepdims=True,
        )
        d_probs = mxu(d_heads, value_heads, CONTRACT_LAST)
        d_scores = (probs * ((d_probs - delta) * scale)).astype(narrow)
        d_query.append(mxu(d_scores, key_heads, CONTRACT_INNER).astype(narrow))
        d_pairs[0].append(mxu(d_scores, queries, CONTRACT_FIRST))
        d_pairs[1].append(mxu(probs_low, d_heads, CONTRACT_FIRST))
    dq_ref[...] = jnp.concatenate(d_query, axis=1)
    for i in range(2):
        total = jnp.concatenate(d_pairs[i], axis=1)
        low_ref[i] = total[:patches].astype(narrow)
        own_ref[i] = total[patches : 2 * patches]
        high_ref[i] = total[2 * patches :].astype(narrow)


def attention_calls(qkv, low, high, seg_rows, seg_keys):
    patches = qkv.shape[1]
    width = qkv.shape[2] // 3
    lanes = GROUP * HEAD_DIM
    groups = width // lanes
    own = [
        pl.BlockSpec((1, patches, lanes), lambda g, i=i: (0, 0, i * groups + g)) for i in range(3)
    ]
    halo = [
        pl.BlockSpec((patches, lanes), lambda g, i=i: (0, i * groups + g)) for i in (0, 1, 0, 1)
    ]
    ids = [
        pl.BlockSpec((patches, 1), lambda g: (0, 0)),
        pl.BlockSpec((1, 3 * patches), lambda g: (0, 0)),
    ]
    operands = (qkv, qkv, qkv, low, low, high, high, seg_rows[:, None], seg_keys[None, :])
    flat = pl.BlockSpec((patches, lanes), lambda g: (0, g))
    stat = pl.BlockSpec((1, patches, GROUP), lambda g: (g, 0, 0))
    pair = pl.BlockSpec((2, patches, lanes), lambda g: (0, 0, g))
    params = pltpu.CompilerParams(vmem_limit_bytes=48 * 1024 * 1024)
    flops = 2 * 3 * patches * patches * width
    exps = 3 * patches * patches * HEADS

    def cost(dots):
        return pl.CostEstimate(
            flops=dots * flops, bytes_accessed=12 * patches * width, transcendentals=exps
        )

    attention, stats = pl.pallas_call(
        forward_kernel,
        grid=(groups,),
        in_specs=own + halo + ids,
        out_specs=(flat, stat),
        out_shape=(
            jax.ShapeDtypeStruct((patches, width), jnp.bfloat16),
            jax.ShapeDtypeStruct((groups, patches, GROUP), jnp.float32),
        ),
        compiler_params=params,
        cost_estimate=cost(2),
        name="attention_forward",
    )(*operands)

    def backward(d_out):
        return pl.pallas_call(
            backward_kernel,
            grid=(groups,),
            in_specs=own + halo + ids + [flat, stat, flat],
            out_specs=(flat, pair, pair, pair),
            out_shape=(
                jax.ShapeDtypeStruct((patches, width), jnp.bfloat16),
                jax.ShapeDtypeStruct((2, patches, width), jnp.bfloat16),
                jax.ShapeDtypeStruct((2, patches, width), jnp.float32),
                jax.ShapeDtypeStruct((2, patches, width), jnp.bfloat16),
            ),
            compiler_params=params,
            cost_estimate=cost(5),
            name="attention_backward",
        )(*operands, attention, stats, d_out)

    return attention, backward


def local(llm_grads, llm_owner, image_ids, stream, ln_gain, pre_act, w_in, w_out, qkv, w_proj):
    single = jnp.float32
    narrow = jnp.bfloat16
    shards = lax.axis_size("cp")
    batches = lax.axis_size("dp")
    device_index = lax.axis_index("cp")
    row_count = llm_grads.shape[1]
    patches = stream.shape[1]
    width = stream.shape[2]
    hidden = w_out.shape[0]
    slot_count = 2 * row_count // shards
    rows = batches * row_count
    packed_width = -(-(hidden + 1) // 128) * 128
    gathered = lax.all_gather(llm_grads[0], "dp", axis=0, tiled=True)
    share = w_proj.shape[0]
    part = share // batches
    own_proj = lax.dynamic_slice_in_dim(w_proj, lax.axis_index("dp") * part, part, 0)
    proj_parts = lax.all_to_all(
        jnp.broadcast_to(own_proj[None], (shards, part, width)),
        "cp",
        split_axis=0,
        concat_axis=0,
        tiled=True,
    ).reshape(shards * part, width)
    proj_parts, key_values, own_owners = lax.optimization_barrier(
        (proj_parts, qkv[0, :, width:], llm_owner[0])
    )
    owners = lax.all_gather(own_owners, "dp", axis=0)
    chip_in = jnp.concatenate([w_in, from_sibling(w_in)], axis=1)
    gathered, proj_parts, owners, chip_in = lax.optimization_barrier(
        (gathered, proj_parts, owners, chip_in)
    )
    full_proj = lax.all_gather(proj_parts, "dp", axis=0, tiled=True)
    low = from_behind(key_values, "cp", 1)
    high = from_behind(key_values, "cp", -1)
    target = owners // row_count
    place = (owners % row_count).reshape(rows, 1)
    same_target = target[:, :, None] == target[:, None, :]
    before = jnp.arange(row_count)[None, :] < jnp.arange(row_count)[:, None]
    rank = jnp.sum((same_target & before[None]).astype(jnp.int32), axis=2)
    batch_of = jnp.arange(batches, dtype=jnp.int32)[:, None]
    slot = ((target * batches + batch_of) * slot_count + rank).reshape(1, rows)
    slots = shards * batches * slot_count
    pick = (jnp.arange(slots, dtype=jnp.int32)[:, None] == slot).astype(narrow)
    d_rows = jnp.dot(gathered, w_out.T, preferred_element_type=single).astype(narrow)
    tags = jnp.where(
        jnp.arange(packed_width - hidden)[None, :] == 0, place + 1, 0
    ).astype(narrow)
    outgoing = jnp.dot(
        pick, jnp.concatenate([d_rows, tags], axis=1), preferred_element_type=single
    ).astype(narrow)
    arrived = lax.all_to_all(
        outgoing.reshape(shards, batches * slot_count, packed_width),
        "cp",
        split_axis=0,
        concat_axis=0,
        tiled=True,
    ).reshape(slots, packed_width)
    arrived, full_proj, low, high = lax.optimization_barrier((arrived, full_proj, low, high))
    tag_row = arrived[:, hidden].astype(jnp.int32).reshape(1, slots)
    slot_batch = (jnp.arange(slots, dtype=jnp.int32) // slot_count % batches)[None, :]
    home = jnp.where(tag_row > 0, slot_batch * row_count + tag_row - 1, -1)
    settle = (jnp.arange(rows, dtype=jnp.int32)[:, None] == home).astype(narrow)
    d_hidden = jnp.dot(settle, arrived, preferred_element_type=single)[:, :hidden].reshape(
        batches, row_count, hidden
    )
    saved_pre = pre_act.astype(single)
    d_pre = (d_hidden * gelu_slope(saved_pre)).astype(narrow)
    halves = d_pre.reshape(batches // 2, 2, row_count, hidden)
    chip_pre = jnp.concatenate(
        [by_core(halves, 1, True), from_sibling(by_core(halves, 1, False))], axis=2
    )
    d_norm = jnp.einsum("bmh,ih->bmi", chip_pre, chip_in, preferred_element_type=single)
    d_norm = d_norm.astype(narrow)
    d_norm = scattered_over_y(d_norm)
    segment = jnp.repeat(image_ids[0], 4)
    seg_rim = jnp.full((patches,), -1, jnp.int32)
    seg_pad = jnp.concatenate([seg_rim, segment, seg_rim], axis=0)
    seg_keys = lax.dynamic_slice_in_dim(seg_pad, device_index * patches, 3 * patches, 0)
    seg_rows = lax.dynamic_slice_in_dim(segment, device_index * patches, patches, 0)
    attention, backward = attention_calls(qkv, low, high, seg_rows, seg_keys)
    column = jnp.arange(width // 2, dtype=jnp.int32)
    column_base = column // part % shards * share + column // (part * shards) * (2 * part)
    column_base = (column_base + column % part)[None, :]
    feature = jnp.arange(width, dtype=jnp.int32)[:, None]
    core = lax.axis_index("dp") % 2

    def features_of(core):
        pick_columns = (feature == column_base + core * part).astype(narrow)
        return jnp.dot(attention, pick_columns, preferred_element_type=single).astype(narrow)

    features = jnp.concatenate([features_of(core), from_sibling(features_of(1 - core))], axis=0)
    stream_wide = stream[0].astype(single)
    inverse = lax.rsqrt(jnp.mean(stream_wide * stream_wide, axis=-1, keepdims=True) + EPS)
    normed = stream_wide * inverse
    d_norm, features = lax.optimization_barrier((d_norm, features))
    d_norm = lax.optimization_barrier(d_norm.reshape(patches, width)).astype(single)
    gain_part = jnp.sum(d_norm * normed, axis=0)
    d_normed = d_norm * ln_gain
    d_stream = (
        inverse * (d_normed - normed * jnp.mean(d_normed * normed, axis=-1, keepdims=True))
    ).astype(narrow)
    d_stream = lax.optimization_barrier(d_stream)
    chip_stream = jnp.concatenate([d_stream, from_sibling(d_stream)], axis=0)
    d_proj_pair = jnp.einsum(
        "pi,pj->ij", features, chip_stream, preferred_element_type=single
    ).astype(narrow)
    d_out = jnp.einsum(
        "pj,ij->pi", d_stream, full_proj, preferred_element_type=single
    ).astype(narrow)
    row = jnp.arange(width, dtype=jnp.int32)
    natural = row // part % shards * share + row // (part * shards) * part + row % part
    order = (natural[:, None] == jnp.arange(width, dtype=jnp.int32)[None, :]).astype(narrow)
    d_out = jnp.dot(d_out, order, preferred_element_type=single).astype(narrow)
    d_proj_pair, d_out = lax.optimization_barrier((d_proj_pair, d_out))
    over_batches = scattered_over_y(d_proj_pair)
    d_query, d_low, d_own, d_high = backward(d_out)
    over_batches, d_query = lax.optimization_barrier((over_batches, d_query))
    from_prev = from_behind(d_high, "cp", 1)
    from_next = from_behind(d_low, "cp", -1)
    spread = jnp.concatenate(
        [
            over_batches.reshape(shards, part, width),
            jnp.broadcast_to(in_parts(gain_part)[None], (shards, 3, width)),
        ],
        axis=1,
    )
    per_shard = lax.all_to_all(spread, "cp", split_axis=0, concat_axis=0, tiled=True)
    d_pairs = (d_own + from_prev.astype(single) + from_next.astype(single)).astype(narrow)
    d_qkv = jnp.concatenate([d_query, d_pairs[0], d_pairs[1]], axis=1)
    totals = jnp.sum(per_shard.astype(single), axis=0)
    own_rows = jnp.concatenate(
        [totals[:part].astype(narrow), in_parts(jnp.sum(totals[part:], axis=0))], axis=0
    )
    whole = lax.all_gather(own_rows, "dp", axis=0).astype(single)
    d_proj = whole[:, :part].reshape(share, width)
    d_gain = jnp.sum(whole[:, part:], axis=(0, 1))
    return (d_stream[None], d_qkv[None], d_proj, d_gain)


def solution(mesh):
    in_specs = (
        P("dp", "cp", None),
        P("dp", "cp"),
        P("dp", None),
        P("dp", "cp", None),
        P(),
        P(None, "cp", "dp"),
        P(None, "dp"),
        P("dp", None),
        P("dp", "cp", None),
        P("cp", None),
    )
    out_specs = (P("dp", "cp", None), P("dp", "cp", None), P("cp", None), P())
    return jax.shard_map(local, mesh=mesh, in_specs=in_specs, out_specs=out_specs, check_vma=False)
```
